32 devices in a mesh: rep: 8 (over z, x), tp: 4 (over y, core).
Axes of the slice: x: 2, y: 2, z: 4, core: 2. Of those that a mesh axis runs over, the one named last changes fastest.
Arguments:
- suffix_source: bfloat16 [8, 384, 4096], P('rep', None, 'tp'), may hold values from -6 to 6
- suffix_accept: bfloat16 [8, 384, 4096], P('rep', None, 'tp'), may hold values from -3 to 3
- suffix_address: bfloat16 [8, 384, 4096], P('rep', None, 'tp'), may hold values from -3 to 3
- guess_lane_source: bfloat16 [16, 16, 4096], P('rep', None, 'tp'), may hold values from -6 to 6
- guess_lane_accept: bfloat16 [16, 16, 4096], P('rep', None, 'tp'), may hold values from -3 to 3
- guess_lane_address: bfloat16 [16, 16, 4096], P('rep', None, 'tp'), may hold values from -3 to 3
- content_map: bfloat16 [4096, 4096], P(None, 'tp'), may hold values from -0.09375 to 0.09375
- forget_shrink_map: bfloat16 [4096, 128], replicated, may hold values from -0.09375 to 0.09375
- forget_expand_map: bfloat16 [128, 4096], P(None, 'tp'), may hold values from -0.35351562 to 0.35351562
- forget_lane_anchor: float32 [4096], P('tp'), may hold values from -12 to -3
- present_boost: float32 [4096], P('tp'), may hold values from -1.5 to 1.5
- content_blend_share: float32 [4096], P('tp'), may hold values from 0 to 1
- forget_blend_share: float32 [4096], P('tp'), may hold values from 0 to 1
- lane_normal_scale: float32 [4096], P('tp'), may hold values from 0.5 to 1.5
- lane_normal_shift: float32 [4096], P('tp'), may hold values from -1.2 to 1.2
- kernel_memory_saved: float32 [16, 64, 4096], P(None, 'rep', 'tp'), may hold values from -6 to 6
- prior_source_saved: bfloat16 [16, 64, 64], P(None, 'rep', 'tp'), may hold values from -6 to 6
- lane_owner: int32 [16], replicated, may hold values from 0 to 15, as said below
- request_spans: int32 [16], replicated, may hold values from 16 to 400, as said below
- admitted_guesses: int32 [16], replicated, may hold values from 0 to 16
Outputs:
- tail_out: bfloat16 [8, 384, 4096], P('rep', None, 'tp')
- draft_out: bfloat16 [16, 16, 4096], P('rep', None, 'tp')
- state_out: float32 [16, 64, 4096], P(None, 'rep', 'tp')
- shift_out: bfloat16 [16, 64, 64], P(None, 'rep', 'tp')
The draws below stay inside these ranges and needn't reach their ends.
Inputs may be any that keep to these rules, and one draw needn't show every extreme that they name: `lane_owner`: a permutation of the request numbers. `request_spans`: exactly 1 request have 16 + 384 tokens and the others 16; a long request is always dealt to a slot s with s % 2 == 0; each aligned block of 8 consecutive groups holds exactly one group whose first slot is long; the tail buffers of groups whose first slot is not long are not read.
All inputs are finite; a program needn't handle non-finite values.
Results may differ from the reference program's by a relative error of at most 0.0051.
The reference program's roundings to bfloat16 on the way count: a program that leaves them out, or rounds other values in their place, can miss the bound.
Values may be sent and summed in bfloat16 or wider, within the bound.
No kernel may reach another device: no remote copies, remote signals or barrier semaphores. Data moves between devices by JAX's collectives and lax.ppermute only.
A program may use at most 128 MiB of HBM per device.

```python
import math
import jax
import jax.numpy as jnp
from jax import lax

HIDDEN_BREADTH = 4096
BLEND_LANES = 64
SUBSPACE_SPAN = 64
DECAY_RANK = 128
DRAFT = 16
TAIL = 384
REQ_DEV = 2
GROUPS = 8
REQS = 16
LONGS = 1


def dealing(key):
    order_req = jax.random.permutation(jax.random.fold_in(key, 11), REQS).astype(jnp.int32)
    offsets = jax.random.randint(jax.random.fold_in(key, 12), (LONGS,), 0, 8, jnp.int32)
    chosen = jnp.arange(LONGS, dtype=jnp.int32) * 8 + offsets
    long_reqs = order_req[chosen * REQ_DEV]
    length_table = jnp.full((REQS,), DRAFT, jnp.int32).at[long_reqs].set(DRAFT + TAIL)
    return (order_req, length_table)


def draw_lane_owner(key, part):
    return dealing(key)[0]


def draw_request_spans(key, part):
    return dealing(key)[1]


def draw_forget_lane_anchor(key, part):
    chain = TAIL + DRAFT
    head_key = jax.random.fold_in(key, 21)
    chan_key = jax.random.fold_in(key, 22)
    place = jax.random.uniform(head_key, (BLEND_LANES, 1), jnp.float32)
    noise = jax.random.uniform(chan_key, (BLEND_LANES, SUBSPACE_SPAN), jnp.float32, -0.5, 0.5)
    base = math.log(1.0 / 40.0) + place * math.log(40.0 / (8.0 * chain))
    return (base + noise).reshape(HIDDEN_BREADTH)


def touch_ends(entries, rng, smallest, largest):
    index_at = [jax.random.randint(jax.random.fold_in(rng, axis), (), 0, length) for axis, length in enumerate(entries.shape)]
    main_axis = entries.shape.index(max(entries.shape))
    beside = index_at[:main_axis] + [(index_at[main_axis] + 1) % entries.shape[main_axis]] + index_at[main_axis + 1:]
    return entries.at[tuple(index_at)].set(smallest).at[tuple(beside)].set(largest)


def block_scale(rng, extent, split, low, top_value):
    factor_of = 1.0
    for position, parts in split:
        steps = jax.random.uniform(jax.random.fold_in(jax.random.fold_in(rng, 6), position), (parts,), jnp.float32, low / len(split), top_value / len(split))
        factor_of = factor_of * jnp.repeat(jnp.exp(steps), extent[position] // parts).reshape((-1,) + (1,) * (len(extent) - 1 - position))
    return factor_of


def centred(own_key, dims, deviation, limit, cuts=(), held_as=jnp.bfloat16):
    factor_of = block_scale(own_key, dims, cuts, -0.22, 0.18) if cuts else 1.0
    drawn = jax.random.normal(own_key, dims, jnp.float32) * deviation * factor_of
    return jnp.minimum(jnp.maximum(drawn, -limit), limit).astype(held_as)


def setup_inputs(seed: int = 0) -> dict:
    splits = jax.random.split(jax.random.key(seed), 21)
    suffix_source = centred(splits[0], (GROUPS, TAIL, HIDDEN_BREADTH), 1.0, 6.0, ((0, 8), (2, 4)))
    suffix_accept = centred(splits[1], (GROUPS, TAIL, HIDDEN_BREADTH), 0.5, 3.0, ((0, 8), (2, 4)))
    suffix_address = centred(splits[2], (GROUPS, TAIL, HIDDEN_BREADTH), 0.5, 3.0, ((0, 8), (2, 4)))
    guess_lane_source = centred(splits[3], (REQS, DRAFT, HIDDEN_BREADTH), 1.0, 6.0, ((0, 8), (2, 4)))
    guess_lane_accept = centred(splits[4], (REQS, DRAFT, HIDDEN_BREADTH), 0.5, 3.0, ((0, 8), (2, 4)))
    guess_lane_address = centred(splits[5], (REQS, DRAFT, HIDDEN_BREADTH), 0.5, 3.0, ((0, 8), (2, 4)))
    content_map = centred(splits[6], (HIDDEN_BREADTH, HIDDEN_BREADTH), HIDDEN_BREADTH ** -0.5, 0.09375, ((1, 4),))
    forget_shrink_map = centred(splits[7], (HIDDEN_BREADTH, DECAY_RANK), HIDDEN_BREADTH ** -0.5, 0.09375)
    forget_expand_map = centred(splits[8], (DECAY_RANK, HIDDEN_BREADTH), (1.0 / DECAY_RANK ** 0.5), 0.35351562, ((1, 4),))
    forget_lane_anchor = draw_forget_lane_anchor(jax.random.fold_in(splits[20], 71), 0)
    present_boost = centred(splits[10], (HIDDEN_BREADTH,), 0.5, 1.5, ((0, 4),), jnp.float32)
    content_blend_share = jnp.clip(1.0 * jax.random.uniform(splits[11], (HIDDEN_BREADTH,), jnp.float32) ** block_scale(splits[11], (HIDDEN_BREADTH,), ((0, 4),), -0.2, 0.2), 0.0, 1.0)
    forget_blend_share = jnp.clip(1.0 * jax.random.uniform(splits[12], (HIDDEN_BREADTH,), jnp.float32) ** block_scale(splits[12], (HIDDEN_BREADTH,), ((0, 4),), -0.2, 0.2), 0.0, 1.0)
    lane_normal_scale = jnp.clip(1.0 + 0.1 * jax.random.normal(splits[13], (HIDDEN_BREADTH,), jnp.float32), 0.5, 1.5)
    lane_normal_shift = centred(splits[14], (HIDDEN_BREADTH,), 0.3, 1.2, ((0, 4),), jnp.float32)
    kernel_memory_saved = centred(splits[15], (REQS, SUBSPACE_SPAN, HIDDEN_BREADTH), 1.0, 6.0, ((1, 8), (2, 4)), jnp.float32)
    prior_source_saved = centred(splits[16], (REQS, SUBSPACE_SPAN, BLEND_LANES), 1.0, 6.0, ((1, 8), (2, 4)))
    lane_owner = draw_lane_owner(jax.random.fold_in(splits[20], 71), 0)
    request_spans = draw_request_spans(jax.random.fold_in(splits[20], 71), 0)
    admitted_guesses = touch_ends(jax.random.randint(splits[19], (REQS,), 0, DRAFT + 1), jax.random.fold_in(splits[19], 1), 0, DRAFT).astype(jnp.int32)
    return dict(suffix_source=suffix_source, suffix_accept=suffix_accept, suffix_address=suffix_address, guess_lane_source=guess_lane_source, guess_lane_accept=guess_lane_accept, guess_lane_address=guess_lane_address, content_map=content_map, forget_shrink_map=forget_shrink_map, forget_expand_map=forget_expand_map, forget_lane_anchor=forget_lane_anchor, present_boost=present_boost, content_blend_share=content_blend_share, forget_blend_share=forget_blend_share, lane_normal_scale=lane_normal_scale, lane_normal_shift=lane_normal_shift, kernel_memory_saved=kernel_memory_saved, prior_source_saved=prior_source_saved, lane_owner=lane_owner, request_spans=request_spans, admitted_guesses=admitted_guesses)


HIGH = lax.Precision.HIGHEST
EPS = 0.00064

def group_norm(answer_collection, lane_normal_scale, lane_normal_shift):
    center = answer_collection - lax.optimization_barrier(jnp.mean(answer_collection, axis=-1, keepdims=True))
    spread = lax.optimization_barrier(jnp.mean(center * center, axis=-1, keepdims=True))
    normed = (center / jnp.sqrt(spread + EPS)).reshape(answer_collection.shape[0], -1)
    return (normed * lane_normal_scale + lane_normal_shift).astype(jnp.bfloat16)

def token_mix(current, previous, mixing):
    present = current.astype(jnp.float32)
    return (present + (previous.astype(jnp.float32) - present) * mixing).astype(jnp.bfloat16)

def project(mixed_value, decay_mixed_input, content_map, forget_shrink_map, forget_expand_map, forget_lane_anchor):
    content_vectors = jnp.dot(mixed_value, content_map, preferred_element_type=jnp.float32).astype(jnp.bfloat16)
    decay_low_rank = jnp.tanh(jnp.dot(decay_mixed_input, forget_shrink_map, preferred_element_type=jnp.float32)).astype(jnp.bfloat16)
    forget_logscale = -jnp.exp(forget_lane_anchor + jnp.dot(decay_low_rank, forget_expand_map, preferred_element_type=jnp.float32))
    return (content_vectors, forget_logscale)

def advance_once(ongoing_memory, accept_vectors, address_vectors, content_vectors, forget_logscale, lanes_boost):
    answer_vectors = jnp.einsum('hi,hij->hj', accept_vectors, ongoing_memory, precision=HIGH)
    answer_vectors = answer_vectors + lax.optimization_barrier(jnp.sum(accept_vectors * lanes_boost * address_vectors, axis=-1, keepdims=True)) * content_vectors
    ongoing_memory = jnp.exp(forget_logscale)[:, :, None] * ongoing_memory + address_vectors[:, :, None] * content_vectors[:, None, :]
    return (ongoing_memory, answer_vectors)

def reference(suffix_source, suffix_accept, suffix_address, guess_lane_source, guess_lane_accept, guess_lane_address, content_map, forget_shrink_map, forget_expand_map, forget_lane_anchor, present_boost, content_blend_share, forget_blend_share, lane_normal_scale, lane_normal_shift, kernel_memory_saved, prior_source_saved, lane_owner, request_spans, admitted_guesses):
    opening_memory = kernel_memory_saved.reshape(REQS, SUBSPACE_SPAN, BLEND_LANES, SUBSPACE_SPAN).transpose(0, 2, 1, 3)
    start_prev = prior_source_saved.transpose(0, 2, 1).reshape(REQS, HIDDEN_BREADTH)
    lanes_boost = present_boost.reshape(BLEND_LANES, SUBSPACE_SPAN)
    slot_long = request_spans[lane_owner] > DRAFT
    long_groups = jnp.nonzero(slot_long[::REQ_DEV], size=LONGS)[0].astype(jnp.int32)

    def divide_lanes(array):
        return array.astype(jnp.float32).reshape(array.shape[0], BLEND_LANES, SUBSPACE_SPAN)

    def prepare(tokens, first):
        previous = jnp.concatenate([first[None], tokens[:-1]], axis=0)
        content_vectors, forget_logscale = project(token_mix(tokens, previous, content_blend_share), token_mix(tokens, previous, forget_blend_share), content_map, forget_shrink_map, forget_expand_map, forget_lane_anchor)
        return (divide_lanes(content_vectors), forget_logscale.reshape(-1, BLEND_LANES, SUBSPACE_SPAN))

    def run_tail(squad_index):
        query_index = lane_owner[squad_index * REQ_DEV]
        tokens = suffix_source[squad_index]
        content_vectors, forget_logscale = prepare(tokens, start_prev[query_index])
        closing_answer, answer_collection = lax.scan(lambda threaded_pair, source_vectors: advance_once(threaded_pair, source_vectors[0], source_vectors[1], source_vectors[2], source_vectors[3], lanes_boost), opening_memory[query_index], (divide_lanes(suffix_accept[squad_index]), divide_lanes(suffix_address[squad_index]), content_vectors, forget_logscale))
        return (group_norm(answer_collection, lane_normal_scale, lane_normal_shift), closing_answer, tokens[-1])
    tail_norm, tail_end, tail_last = lax.map(run_tail, long_groups)
    tail_out = jnp.zeros((GROUPS, TAIL, HIDDEN_BREADTH), jnp.bfloat16).at[long_groups].set(tail_norm)
    end_by_group = jnp.zeros((GROUPS, BLEND_LANES, SUBSPACE_SPAN, SUBSPACE_SPAN), jnp.float32).at[long_groups].set(tail_end)
    last_by_group = jnp.zeros((GROUPS, HIDDEN_BREADTH), jnp.bfloat16).at[long_groups].set(tail_last)

    def run_draft(slot):
        query_index = lane_owner[slot]
        squad_index = slot // REQ_DEV
        trailing_pair = jnp.where(slot_long[slot], end_by_group[squad_index], opening_memory[query_index])
        first = jnp.where(slot_long[slot], last_by_group[squad_index], start_prev[query_index])
        tokens = guess_lane_source[slot]
        content_vectors, forget_logscale = prepare(tokens, first)
        count = admitted_guesses[query_index]

        def advance(threaded_pair, source_vectors):
            ongoing_memory, chosen = threaded_pair
            ongoing_memory, answer_vectors = advance_once(ongoing_memory, source_vectors[0], source_vectors[1], source_vectors[2], source_vectors[3], lanes_boost)
            chosen = jnp.where(source_vectors[4] + 1 == count, ongoing_memory, chosen)
            return ((ongoing_memory, chosen), answer_vectors)
        positions = jnp.arange(DRAFT, dtype=jnp.int32)
        (final_state, chosen), answer_collection = lax.scan(advance, (trailing_pair, trailing_pair), (divide_lanes(guess_lane_accept[slot]), divide_lanes(guess_lane_address[slot]), content_vectors, forget_logscale, positions))
        edge = jnp.where(count > 0, tokens[jnp.maximum(count - 1, 0)], first)
        return (group_norm(answer_collection, lane_normal_scale, lane_normal_shift), chosen, edge)
    draft_out, chosen, edges = lax.map(run_draft, jnp.arange(REQS, dtype=jnp.int32))
    by_request = jnp.zeros_like(chosen).at[lane_owner].set(chosen)
    state_out = by_request.transpose(0, 2, 1, 3).reshape(REQS, SUBSPACE_SPAN, HIDDEN_BREADTH)
    shift_out = jnp.zeros_like(edges).at[lane_owner].set(edges).reshape(REQS, BLEND_LANES, SUBSPACE_SPAN).transpose(0, 2, 1)
    return (tail_out, draft_out, state_out, shift_out)
```

```python
import functools

import jax
import jax.numpy as jnp
from jax import lax
from jax.experimental import pallas as pl
from jax.experimental.pallas import tpu as pltpu
from jax.sharding import PartitionSpec as P

SPAN = 64
DRAFT = 16
PAIR = 2 * SPAN
CHUNK = 64
PIECES = 3
EXTRA = 16
TAIL_FIRST, TAIL_LAST, MIX_V, MIX_W = 0, 1, 2, 5
EPS = 0.00064
SAFE = -60.0
F32, BF16 = jnp.float32, jnp.bfloat16
VMEM_BYTES = 40 * 1024 * 1024
VMEM = pl.BlockSpec(memory_space=pltpu.VMEM)
SMEM = pl.BlockSpec(memory_space=pltpu.SMEM)
ANYWHERE = pl.BlockSpec(memory_space=pl.ANY)


def params():
    return pltpu.CompilerParams(vmem_limit_bytes=VMEM_BYTES)


def iota(shape, dim):
    return lax.broadcasted_iota(jnp.int32, shape, dim)


def split2(x):
    high = x.astype(BF16)
    return high, (x - high.astype(F32)).astype(BF16)


def split3(x):
    high = x.astype(BF16)
    rest = x - high.astype(F32)
    mid = rest.astype(BF16)
    return high, mid, (rest - mid.astype(F32)).astype(BF16)


def dot(a, b):
    return jnp.dot(a, b, preferred_element_type=F32)


def dot_rows(a, b):
    return lax.dot_general(a, b, (((0,), (0,)), ((), ())), preferred_element_type=F32)


def dot_lanes(a, b):
    return lax.dot_general(a, b, (((1,), (1,)), ((), ())), preferred_element_type=F32)


def pack_kernel(
    slots,
    owner,
    state,
    prior,
    draft,
    head,
    foot,
    mix_v,
    mix_w,
    state_out,
    prior_out,
    small_out,
):
    groups = state_out.shape[0]
    copies = prior_out.shape[0] // groups
    heads = prior.shape[2]
    place_row, place_lane = iota((heads, 128), 0), iota((heads, 128), 1)
    for g in range(groups):
        reqs = [owner[g * slots + s] for s in range(slots)]
        rows = jnp.concatenate([state[q] for q in reqs], axis=0)
        state_out[g] = rows.astype(BF16)
        spread = sum(
            dot(prior[q], (place_lane == place_row + s * heads).astype(BF16))
            for s, q in enumerate(reqs)
        )
        for c in range(copies):
            prior_out[g * copies + c] = spread
    for s in range(slots):
        small_out[s * DRAFT : (s + 1) * DRAFT, :] = draft[s]
    width = small_out.shape[1]
    row = iota((EXTRA, width), 0)
    rest = jnp.where(row == TAIL_FIRST, head[...].astype(F32)[0:1], 0.0)
    rest = jnp.where(row == TAIL_LAST, foot[...].astype(F32)[EXTRA - 1 : EXTRA], rest)
    for base, share in ((MIX_V, mix_v), (MIX_W, mix_w)):
        for n, part in enumerate(split3(share[...])):
            rest = jnp.where(row == base + n, part.astype(F32), rest)
    small_out[slots * DRAFT :, :] = rest.astype(BF16)


def pack(lane_owner, state, prior, draft, tail, mix_v, mix_w, groups, copies):
    reqs, lines, width = state.shape
    slots = draft.shape[0]
    last = tail.shape[0] // EXTRA - 1
    whole = lambda *shape: pl.BlockSpec(shape, lambda i: (0,) * len(shape))
    return pl.pallas_call(
        functools.partial(pack_kernel, slots),
        grid=(1,),
        in_specs=[
            SMEM,
            whole(*state.shape),
            whole(*prior.shape),
            whole(*draft.shape),
            pl.BlockSpec((EXTRA, width), lambda i: (0, 0)),
            pl.BlockSpec((EXTRA, width), lambda i: (last, 0)),
            whole(1, width),
            whole(1, width),
        ],
        out_specs=[
            whole(groups, slots * lines, width),
            whole(groups * copies, lines, 128),
            whole(slots * DRAFT + EXTRA, width),
        ],
        out_shape=[
            jax.ShapeDtypeStruct((groups, slots * lines, width), BF16),
            jax.ShapeDtypeStruct((groups * copies, lines, 128), F32),
            jax.ShapeDtypeStruct((slots * DRAFT + EXTRA, width), BF16),
        ],
        compiler_params=params(),
        name="pack",
    )(lane_owner, state, prior, draft, tail, tail, mix_v, mix_w)


def prior_row(prior, block, copies, slot, heads, width):
    groups = prior.shape[0] // copies
    lines = jnp.concatenate([prior[g * copies + block] for g in range(groups)], axis=0)
    lane = iota((128, width), 1)
    place = (iota((128, width), 0) == slot * heads + lane // SPAN).astype(BF16)
    spread = dot(lines.astype(BF16), place)
    keep = iota((SPAN, width), 0) == iota((SPAN, width), 1) % SPAN
    return jnp.sum(jnp.where(keep, spread, 0.0), axis=0, keepdims=True)


def mixed(x, previous, share):
    return (x + (previous - x) * share).astype(BF16)


def project_kernel(slots, copies, has_before, has_draft, *refs):
    refs = list(refs)
    take = lambda n: [refs.pop(0) for _ in range(n)]
    owner, spans = take(2)
    xs = take(copies)
    before = take(copies) if has_before else None
    smalls = take(copies)
    shrink, expand, anchor, weights = take(4)
    prior = take(1)[0] if has_draft else None
    v_out, w_out = take(2)
    vd_out, wd_out = take(2) if has_draft else (None, None)
    acc_v, acc_w, held, sems = take(4)
    width = v_out.shape[1]
    rows = v_out.shape[0]
    drafts = slots * DRAFT
    me = lax.axis_index("tp")
    blocks = [jnp.bitwise_xor(me, j) for j in range(copies)]

    def fetch(j):
        start = pl.multiple_of(blocks[j] * width, width)
        return pltpu.make_async_copy(weights.at[pl.ds(start, width), :], held.at[j], sems.at[j])

    for j in range(copies):
        fetch(j).start()
    if has_draft:
        first_slot = lax.axis_index("rep") * slots
        is_long = [spans[owner[first_slot + s]] > DRAFT for s in range(slots)]
    for j in range(copies):
        x = xs[j][...].astype(F32)
        row = iota(x.shape, 0)
        previous = pltpu.roll(x, 1, 0)
        if has_before:
            previous = jnp.where(row == 0, before[j][...].astype(F32)[EXTRA - 1 : EXTRA], previous)
        rest = smalls[j][drafts:, :].astype(F32)
        share_v = rest[MIX_V : MIX_V + 1] + rest[MIX_V + 1 : MIX_V + 2] + rest[MIX_V + 2 : MIX_V + 3]
        share_w = rest[MIX_W : MIX_W + 1] + rest[MIX_W + 1 : MIX_W + 2] + rest[MIX_W + 2 : MIX_W + 3]
        xv, xw = mixed(x, previous, share_v), mixed(x, previous, share_w)
        if has_draft:
            d = smalls[j][...].astype(F32)
            row = iota(d.shape, 0)
            previous = pltpu.roll(d, 1, 0)
            for s in range(slots):
                prior_first = prior_row(prior, blocks[j], copies, s, width // SPAN, width)
                first = jnp.where(is_long[s], rest[TAIL_LAST : TAIL_LAST + 1], prior_first)
                previous = jnp.where(row == s * DRAFT, first, previous)
                if s == 0:
                    previous = jnp.where(row == drafts + TAIL_FIRST, prior_first, previous)
            xv = jnp.concatenate([xv, mixed(d, previous, share_v)], axis=0)
            xw = jnp.concatenate([xw, mixed(d, previous, share_w)], axis=0)
        low = dot(xw, shrink[pl.ds(pl.multiple_of(blocks[j] * width, width), width), :])
        fetch(j).wait()
        part = dot(xv, held[j])
        if j == 0:
            acc_w[...] = low
            acc_v[...] = part
        else:
            acc_w[...] += low
            acc_v[...] += part
    rate = -jnp.exp(anchor[...] + dot(jnp.tanh(acc_w[...]).astype(BF16), expand[...]))
    v_out[...] = acc_v[0:rows, :].astype(BF16)
    w_out[...] = rate[0:rows]
    if has_draft:
        vd_out[...] = acc_v[rows:, :].astype(BF16)
        wd_out[...] = rate[rows:]


def project(
    piece,
    lane_owner,
    spans,
    wholes,
    parts,
    befores,
    smalls,
    shrink,
    expand,
    anchor,
    weights,
    prior,
    slots,
    rows,
):
    copies = len(smalls)
    width = weights.shape[1]
    drafts = smalls[0].shape[0]
    whole = lambda shape: pl.BlockSpec(shape, lambda i: (0,) * len(shape))
    has_before, has_draft = piece > 0, prior is not None
    per = rows // EXTRA
    in_specs = [SMEM, SMEM]
    in_specs += [pl.BlockSpec((rows, width), lambda i: (piece, 0)) for _ in wholes]
    in_specs += [whole((rows, width)) for _ in parts]
    args = [lane_owner, spans, *wholes, *parts]
    if has_before:
        in_specs += [pl.BlockSpec((EXTRA, width), lambda i: (piece * per - 1, 0)) for _ in wholes]
        in_specs += [pl.BlockSpec((EXTRA, width), lambda i: (per - 1, 0)) for _ in befores]
        args += [*wholes, *befores]
    for array in (*smalls, shrink, expand, anchor):
        in_specs.append(whole(array.shape))
        args.append(array)
    in_specs.append(ANYWHERE)
    args.append(weights)
    outs = [((rows, width), BF16), ((rows, width), F32)]
    total = rows
    if has_draft:
        in_specs.append(whole(prior.shape))
        args.append(prior)
        outs += [((drafts, width), BF16), ((drafts, width), F32)]
        total += drafts
    return pl.pallas_call(
        functools.partial(project_kernel, slots, copies, has_before, has_draft),
        grid=(1,),
        in_specs=in_specs,
        out_specs=[whole(s) for s, _ in outs],
        out_shape=[jax.ShapeDtypeStruct(s, t) for s, t in outs],
        scratch_shapes=[
            pltpu.VMEM((total, width), F32),
            pltpu.VMEM((total, shrink.shape[1]), F32),
            pltpu.VMEM((copies, width, width), BF16),
            pltpu.SemaphoreType.DMA((copies,)),
        ],
        compiler_params=params(),
        cost_estimate=pl.CostEstimate(
            flops=2 * total * weights.shape[0] * width,
            bytes_accessed=2 * weights.shape[0] * width,
            transcendentals=0,
        ),
        name=f"project_{piece}",
    )(*args)


def lane_low(shape):
    return iota(shape, 1) < SPAN


def by_head(x):
    low = lane_low(x.shape)
    return jnp.concatenate([jnp.where(low, x, 0.0), jnp.where(low, 0.0, x)], axis=0)


def head_sum(x):
    high, low = split2(x)
    r, c = iota((2 * PAIR, PAIR), 0), iota((2 * PAIR, PAIR), 1)
    same = ((r // SPAN) % 2 == c // SPAN).astype(BF16)
    return dot(jnp.concatenate([high, low], axis=1), same)


def down(line):
    return jnp.transpose(jnp.broadcast_to(line, (PAIR, PAIR)))


def per_segment(lines, length):
    if len(lines) == 1:
        return lines[0]
    return jnp.concatenate([jnp.broadcast_to(x, (length, x.shape[1])) for x in lines], axis=0)


def running(rate, length):
    n = rate.shape[0]
    t, s = iota((n, 3 * n), 0), iota((n, 3 * n), 1) % n
    upto = ((s <= t) & (s // length == t // length)).astype(BF16)
    return dot(upto, jnp.concatenate(split3(rate), axis=0))


def scores_scaled(r, k, rate, inclusive, middle, length):
    n = r.shape[0]
    rt = r * jnp.exp(inclusive - rate - middle)
    kt = k * jnp.exp(middle - inclusive)
    sc = dot_lanes(by_head(rt).astype(BF16), kt.astype(BF16))
    t, s = iota((2 * n, n), 0) % n, iota((2 * n, n), 1)
    return jnp.where((s < t) & (s // length == t // length), sc, 0.0)


def scores_levels(r, k, rate, length):
    n = r.shape[0]
    pieces = split3(rate)
    levels = length.bit_length() - 1

    def level(n_level, total):
        half = lax.shift_left(jnp.int32(1), n_level)
        shift = n_level + 1
        t, u = iota((n, 3 * n), 0), iota((n, 3 * n), 1) % n
        edge = lax.shift_left(lax.shift_right_logical(t, shift), shift) + half
        after = (t >= edge) & (u >= edge) & (u < t)
        ahead = (t < edge) & (u > t) & (u < edge)
        decay = jnp.exp(dot((after | ahead).astype(BF16), jnp.concatenate(pieces, axis=0)))
        row = iota(r.shape, 0)
        row_edge = lax.shift_left(lax.shift_right_logical(row, shift), shift) + half
        rt = jnp.where(row >= row_edge, r * decay, 0.0)
        kt = jnp.where(row < row_edge, k * decay, 0.0)
        sc = dot_lanes(by_head(rt).astype(BF16), kt.astype(BF16))
        t2, s2 = iota((2 * n, n), 0) % n, iota((2 * n, n), 1)
        same = lax.shift_right_logical(t2, shift) == lax.shift_right_logical(s2, shift)
        return total + jnp.where(same, sc, 0.0)

    return lax.fori_loop(0, levels, level, jnp.zeros((2 * n, n), F32))


def answers(r, k, v, rate, boost, states, length, scaled):
    n = r.shape[0]
    count = n // length
    inclusive = running(rate, length)
    if scaled:
        middle = per_segment(
            [inclusive[s * length + length // 2 : s * length + length // 2 + 1] for s in range(count)],
            length,
        )
        sc = scores_scaled(r, k, rate, inclusive, middle, length)
    else:
        sc = scores_levels(r, k, rate, length)
    inner = dot(sc.astype(BF16), v)
    y = jnp.where(lane_low((n, PAIR)), inner[:n], inner[n:])
    rs = (r * jnp.exp(inclusive - rate)).astype(BF16)
    outer = [dot(rs[s * length : (s + 1) * length], states[s].astype(BF16)) for s in range(count)]
    y = y + (outer[0] if count == 1 else jnp.concatenate(outer, axis=0))
    y = y + head_sum(r * k * boost) * v.astype(F32)
    return y, inclusive


def gathered(keys, v):
    high, low = split2(keys)
    full = dot_rows(jnp.concatenate([high, low], axis=0), jnp.concatenate([v, v], axis=0))
    same = (iota((PAIR, PAIR), 0) < SPAN) == (iota((PAIR, PAIR), 1) < SPAN)
    return jnp.where(same, full, 0.0)


def normed(y, gain, bias):
    center = y - head_sum(y) * (1.0 / SPAN)
    spread = head_sum(center * center) * (1.0 / SPAN)
    return (center * lax.rsqrt(spread + EPS) * gain + bias).astype(BF16)


def mix_kernel(slots, copies, direct, *refs):
    refs = list(refs)
    take = lambda n: [refs.pop(0) for _ in range(n)]
    owner, spans, admitted = take(3)
    vs, ws = take(PIECES), take(PIECES)
    v_draft, w_draft, r_tail, k_tail, r_draft, k_draft, got, small, prior = take(9)
    boost, gain, bias = take(3)
    tail_out, draft_out, back = take(3)
    v_all, w_all, states = take(3)
    width = v_all.shape[1]
    pairs = width // PAIR
    rows = vs[0].shape[0]
    total = rows * PIECES
    drafts = slots * DRAFT
    first_slot = lax.axis_index("rep") * slots
    reqs = [owner[first_slot + s] for s in range(slots)]
    is_long = [spans[q] > DRAFT for q in reqs]
    me = lax.axis_index("tp")

    groups = got.shape[0]
    lines = SPAN // groups
    for s in range(slots):
        begin = jnp.concatenate(
            [got[g].astype(F32)[s * lines : (s + 1) * lines] for g in range(groups)], axis=0
        )
        for p in range(pairs):
            b = begin[:, p * PAIR : (p + 1) * PAIR]
            low = lane_low(b.shape)
            states[s, p] = jnp.concatenate([jnp.where(low, b, 0.0), jnp.where(low, 0.0, b)], axis=0)

    def chunk_pair(c, p, scaled):
        at = pl.ds(pl.multiple_of(c * CHUNK, CHUNK), CHUNK)
        lanes = pl.ds(p * PAIR if isinstance(p, int) else pl.multiple_of(p * PAIR, PAIR), PAIR)
        r, k = r_tail[at, lanes].astype(F32), k_tail[at, lanes].astype(F32)
        v, rate = v_all[at, lanes], w_all[at, lanes]
        state = states[0, p]
        y, inclusive = answers(r, k, v, rate, boost[:, lanes], [state], CHUNK, scaled)
        closing = inclusive[CHUNK - 1 : CHUNK]
        states[0, p] = down(jnp.exp(closing)) * state + gathered(k * jnp.exp(closing - inclusive), v)
        tail_out[at, lanes] = normed(y, gain[:, lanes], bias[:, lanes])

    @pl.when(is_long[0])
    def _():
        lowest = jnp.zeros((1, width), F32)
        for n in range(PIECES):
            v, w = vs[n][...], ws[n][...]
            if n == 0:
                row = iota(w.shape, 0)
                start = drafts + TAIL_FIRST
                w = jnp.where(row == 0, w_draft[...][start : start + 1], w)
                v = jnp.where(row == 0, v_draft[...].astype(F32)[start : start + 1], v.astype(F32)).astype(BF16)
            v_all[n * rows : (n + 1) * rows, :] = v
            w_all[n * rows : (n + 1) * rows, :] = w
            for c in range(rows // CHUNK):
                lowest = jnp.minimum(
                    lowest, jnp.sum(w[c * CHUNK : (c + 1) * CHUNK], axis=0, keepdims=True)
                )
        safe = jnp.min(lowest) > SAFE

        @pl.when(safe)
        def _():
            def body(c, carry):
                for p in range(pairs):
                    chunk_pair(c, p, True)
                return carry

            lax.fori_loop(0, total // CHUNK, body, 0)

        @pl.when(jnp.logical_not(safe))
        def _():
            def body(n, carry):
                chunk_pair(n // pairs, n % pairs, False)
                return carry

            lax.fori_loop(0, total // CHUNK * pairs, body, 0)

    @pl.when(jnp.logical_not(is_long[0]))
    def _():
        tail_out[...] = jnp.zeros_like(tail_out)

    counts = [admitted[q] for q in reqs]
    lowest = jnp.min(
        jnp.concatenate(
            [
                jnp.sum(w_draft[s * DRAFT : (s + 1) * DRAFT, :], axis=0, keepdims=True)
                for s in range(slots)
            ],
            axis=0,
        )
    )
    safe = lowest > SAFE

    def draft_pair(p, scaled):
        lanes = pl.ds(p * PAIR if isinstance(p, int) else pl.multiple_of(p * PAIR, PAIR), PAIR)
        r, k = r_draft[:, lanes].astype(F32), k_draft[:, lanes].astype(F32)
        v, rate = v_draft[0:drafts, lanes], w_draft[0:drafts, lanes]
        begin = [states[s, p] for s in range(slots)]
        y, inclusive = answers(r, k, v, rate, boost[:, lanes], begin, DRAFT, scaled)
        draft_out[:, lanes] = normed(y, gain[:, lanes], bias[:, lanes])
        row = iota((drafts, PAIR), 0)
        ends = []
        for s in range(slots):
            taken = (row >= s * DRAFT) & (row < s * DRAFT + counts[s])
            upto = jnp.sum(jnp.where(taken, rate, 0.0), axis=0, keepdims=True)
            weight = jnp.where(taken, jnp.exp(jnp.minimum(upto - inclusive, 0.0)), 0.0)
            end = down(jnp.exp(upto)) * begin[s] + gathered(k * weight, v)
            ends.append(end[:SPAN] + end[SPAN:])
        if direct:
            for g in range(groups):
                part = jnp.concatenate([e[g * lines : (g + 1) * lines] for e in ends], axis=0)
                back[g, :, lanes] = part.astype(BF16)
        else:
            for s in range(slots):
                back[s, :, lanes] = ends[s].astype(BF16)

    @pl.when(safe)
    def _():
        for p in range(pairs):
            draft_pair(p, True)

    @pl.when(jnp.logical_not(safe))
    def _():
        def body(p, carry):
            draft_pair(p, False)
            return carry

        lax.fori_loop(0, pairs, body, 0)

    heads = width // SPAN
    tokens = small[...].astype(F32)
    row = iota((drafts + EXTRA, width), 0)
    place = (iota((128, width), 0) == iota((128, width), 1) // SPAN).astype(BF16)
    keep = iota((SPAN, width), 0) == iota((SPAN, width), 1) % SPAN
    edges = []
    for s in range(slots):
        own = prior_row(prior, me, copies, s, heads, width)
        last = drafts + TAIL_LAST
        first = jnp.where(is_long[s], tokens[last : last + 1], own)
        chosen = jnp.sum(jnp.where(row == s * DRAFT + counts[s] - 1, tokens, 0.0), axis=0, keepdims=True)
        edge = jnp.where(counts[s] > 0, chosen, first)
        edges.append(dot_lanes(jnp.where(keep, edge, 0.0).astype(BF16), place))
    if direct:
        for g in range(groups):
            part = jnp.concatenate([e[g * lines : (g + 1) * lines] for e in edges], axis=0)
            back[g, :, width:] = part.astype(BF16)
    else:
        for s in range(slots):
            back[s, :, width:] = edges[s].astype(BF16)


def time_mix(scalars, vs, ws, arrays, slots, copies):
    width = vs[0].shape[1]
    rows = vs[0].shape[0]
    got = arrays[6]
    groups = got.shape[0]
    direct = SPAN // groups == 8
    back = (groups, slots * SPAN // groups) if direct else (slots, SPAN)
    back = (*back, width + 128)
    outs = [((rows * PIECES, width), BF16), ((slots * DRAFT, width), BF16), (back, BF16)]
    tail_out, draft_out, ret = pl.pallas_call(
        functools.partial(mix_kernel, slots, copies, direct),
        in_specs=[SMEM] * len(scalars) + [VMEM] * (2 * PIECES + len(arrays)),
        out_specs=[VMEM] * 3,
        out_shape=[jax.ShapeDtypeStruct(s, t) for s, t in outs],
        scratch_shapes=[
            pltpu.VMEM((rows * PIECES, width), BF16),
            pltpu.VMEM((rows * PIECES, width), F32),
            pltpu.VMEM((slots, width // PAIR, PAIR, PAIR), F32),
        ],
        compiler_params=params(),
        name="time_mix",
    )(*scalars, *vs, *ws, *arrays)
    if not direct:
        lines = SPAN // groups
        ret = ret.reshape(slots, groups, lines, width + 128).transpose(1, 0, 2, 3)
        ret = ret.reshape(groups, slots * lines, width + 128)
    return tail_out, draft_out, ret


def unpack_kernel(slots, owner, back, state_out, shift_out):
    reqs, lines, width = state_out.shape
    heads = shift_out.shape[2]
    for g in range(reqs // slots):
        rows = back[g].astype(F32)
        for s in range(slots):
            q = owner[g * slots + s]
            mine = rows[s * lines : (s + 1) * lines]
            state_out[q] = mine[:, :width]
            shift_out[q] = mine[:, width : width + heads].astype(BF16)


def unpack(lane_owner, back, slots, lines, width, heads):
    reqs = back.shape[0] * slots
    return pl.pallas_call(
        functools.partial(unpack_kernel, slots),
        in_specs=[SMEM, VMEM],
        out_specs=[VMEM, VMEM],
        out_shape=[
            jax.ShapeDtypeStruct((reqs, lines, width), F32),
            jax.ShapeDtypeStruct((reqs, lines, heads), BF16),
        ],
        compiler_params=params(),
        name="unpack",
    )(lane_owner, back)


def local(
    groups,
    copies,
    suffix_source,
    suffix_accept,
    suffix_address,
    guess_lane_source,
    guess_lane_accept,
    guess_lane_address,
    content_map,
    forget_shrink_map,
    forget_expand_map,
    forget_lane_anchor,
    present_boost,
    content_blend_share,
    forget_blend_share,
    lane_normal_scale,
    lane_normal_shift,
    kernel_memory_saved,
    prior_source_saved,
    lane_owner,
    request_spans,
    admitted_guesses,
):
    width = content_map.shape[1]
    slots = guess_lane_source.shape[0]
    drafts = slots * DRAFT
    lines = kernel_memory_saved.shape[1]
    line = lambda x: x.reshape(1, width)

    def flip(x, k):
        return lax.ppermute(x, "tp", [(i, i ^ k) for i in range(copies)])

    tail = suffix_source[0]
    rows = tail.shape[0] // PIECES
    state_sent, prior_sent, small = pack(
        lane_owner,
        kernel_memory_saved,
        prior_source_saved,
        guess_lane_source,
        tail,
        line(content_blend_share),
        line(forget_blend_share),
        groups,
        copies,
    )
    cross = [flip(tail[n * rows : (n + 1) * rows], 2) for n in range(PIECES)]
    near = flip(tail, 1)
    smalls = [small] + [flip(small, k) for k in range(1, copies)]
    got = lax.all_to_all(state_sent, "rep", 0, 0)
    prior = lax.all_to_all(prior_sent, ("rep", "tp"), 0, 0)
    far = [flip(x, 1) for x in cross]
    vs, ws = [], []
    for n in range(PIECES):
        out = project(
            n,
            lane_owner,
            request_spans,
            [tail, near],
            [cross[n], far[n]],
            [cross[n - 1], far[n - 1]] if n else [],
            smalls,
            forget_shrink_map,
            forget_expand_map,
            line(forget_lane_anchor),
            content_map,
            prior if n == PIECES - 1 else None,
            slots,
            rows,
        )
        vs.append(out[0])
        ws.append(out[1])
    v_draft, w_draft = out[2:]
    tail_out, draft_out, ret = time_mix(
        (lane_owner, request_spans, admitted_guesses),
        vs,
        ws,
        (
            v_draft,
            w_draft,
            suffix_accept[0],
            suffix_address[0],
            guess_lane_accept.reshape(drafts, width),
            guess_lane_address.reshape(drafts, width),
            got,
            small,
            prior,
            line(present_boost),
            line(lane_normal_scale),
            line(lane_normal_shift),
        ),
        slots,
        copies,
    )
    back = lax.all_to_all(ret, "rep", 0, 0)
    state_out, shift_out = unpack(lane_owner, back, slots, lines, width, width // SPAN)
    return (
        tail_out[None],
        draft_out.reshape(slots, DRAFT, width),
        state_out,
        shift_out,
    )


def solution(mesh):
    wide = P("rep", None, "tp")
    cached = P(None, "rep", "tp")
    placed = (wide,) * 6 + (P(None, "tp"), P(), P(None, "tp")) + (P("tp"),) * 6
    placed += (cached, cached, P(), P(), P())
    return jax.shard_map(
        functools.partial(local, mesh.shape["rep"], mesh.shape["tp"]),
        mesh=mesh,
        in_specs=placed,
        out_specs=(wide, wide, cached, cached),
        check_vma=False,
    )
```

```python
import functools

import jax
import jax.numpy as jnp
from jax import lax
from jax.experimental import pallas as pl
from jax.experimental.pallas import tpu as pltpu
from jax.sharding import PartitionSpec as P

SPAN = 64
DRAFT = 16
QUAD = 4 * SPAN
PIECES = 3
LINE = 128
EXTRA = 16
TAIL_FIRST, TAIL_LAST, MIX_V, MIX_W, PRIOR = 0, 1, 2, 5, 8
EPS = 0.00064
SAFE = -60.0
F32, BF16 = jnp.float32, jnp.bfloat16
VMEM_BYTES = 62 * 1024 * 1024
SMEM = pl.BlockSpec(memory_space=pltpu.SMEM)
HBM = pl.BlockSpec(memory_space=pltpu.HBM)


def params():
    return pltpu.CompilerParams(vmem_limit_bytes=VMEM_BYTES)


def iota(shape, dim):
    return lax.broadcasted_iota(jnp.int32, shape, dim)


def split2(x, axis):
    high = x.astype(BF16)
    return jnp.concatenate([high, (x - high.astype(F32)).astype(BF16)], axis=axis)


def split3(x):
    high = x.astype(BF16)
    rest = x - high.astype(F32)
    mid = rest.astype(BF16)
    return high, mid, (rest - mid.astype(F32)).astype(BF16)


def dot(a, b):
    return jnp.dot(a, b, preferred_element_type=F32)


def dot_rows(a, b):
    return lax.dot_general(a, b, (((0,), (0,)), ((), ())), preferred_element_type=F32)


def dot_lanes(a, b):
    return lax.dot_general(a, b, (((1,), (1,)), ((), ())), preferred_element_type=F32)


def quad_lanes(p):
    if isinstance(p, int):
        return slice(p * QUAD, (p + 1) * QUAD)
    return pl.ds(pl.multiple_of(p * QUAD, QUAD), QUAD)


class Copies:
    def __init__(self, sems):
        self.sems, self.used = sems, 0

    def start(self, source, target):
        copy = pltpu.make_async_copy(source, target, self.sems.at[self.used])
        self.used += 1
        copy.start()
        return copy


def call(kernel, args, in_specs, outs, scratch, name, flops=0, moved=0, out_specs=None):
    return pl.pallas_call(
        kernel,
        in_specs=in_specs,
        out_specs=out_specs or [HBM] * len(outs),
        out_shape=[jax.ShapeDtypeStruct(s, t) for s, t in outs],
        scratch_shapes=scratch,
        compiler_params=params(),
        cost_estimate=pl.CostEstimate(flops=flops, bytes_accessed=moved, transcendentals=0),
        name=name,
    )(*args)


def mix_rows(row, mix_v, mix_w):
    value = jnp.zeros(row.shape, F32)
    for base, share in ((MIX_V, mix_v), (MIX_W, mix_w)):
        for m, part in enumerate(split3(share)):
            value = jnp.where(row == base + m, part.astype(F32), value)
    return value


def pack_kernel(slots, owner, state, prior, mix_v, mix_w, out, mixes, held, cached, lines, lanes, sems):
    groups, rows, _ = out.shape
    width = state.shape[2]
    heads = prior.shape[2]
    go = Copies(sems)
    second = go.start(state, held)
    first = [go.start(prior, cached), go.start(mix_v, lanes.at[0]), go.start(mix_w, lanes.at[1])]
    lines[...] = jnp.zeros_like(lines)
    for w in first:
        w.wait()
    lines[:, :, 0:heads] = cached[...].astype(F32)
    mixes[...] = mix_rows(iota(mixes.shape, 0), lanes[0], lanes[1]).astype(BF16)
    second.wait()
    for g in range(groups):
        reqs = [owner[g * slots + s] for s in range(slots)]
        out[g, :, 0:width] = jnp.concatenate([held[q] for q in reqs], axis=0).astype(BF16)
        out[g, :, width:] = jnp.concatenate([lines[q] for q in reqs], axis=0).astype(BF16)


def pack(lane_owner, state, prior, mix_v, mix_w, groups):
    reqs, depth, width = state.shape
    slots = reqs // groups
    outs = [(groups, slots * depth, width + LINE), (EXTRA, width)]
    whole = lambda *shape: pl.BlockSpec(shape, lambda i: (0,) * len(shape))
    return pl.pallas_call(
        functools.partial(pack_kernel, slots),
        grid=(1,),
        in_specs=[SMEM] + [HBM] * 4,
        out_specs=[whole(*o) for o in outs],
        out_shape=[jax.ShapeDtypeStruct(o, BF16) for o in outs],
        scratch_shapes=[
            pltpu.VMEM(state.shape, F32),
            pltpu.VMEM(prior.shape, BF16),
            pltpu.VMEM((reqs, depth, LINE), F32),
            pltpu.VMEM((2, 1, width), F32),
            pltpu.SemaphoreType.DMA((4,)),
        ],
        compiler_params=params(),
        name="pack",
    )(lane_owner, state, prior, mix_v, mix_w)


def small_kernel(slots, draft, tail, mixes, got, small, ends, lines, held, sems):
    copies = Copies(sems)
    last = tail.shape[0] - 16
    drafts = slots * DRAFT
    width = held.shape[1]
    waits = [
        copies.start(tail.at[pl.ds(0, 16), :], ends.at[0]),
        copies.start(tail.at[pl.ds(last, 16), :], ends.at[1]),
        copies.start(mixes, ends.at[2]),
        copies.start(got.at[:, :, pl.ds(width, LINE)], lines),
    ]
    waits += [copies.start(draft.at[s], held.at[pl.ds(s * DRAFT, DRAFT), :]) for s in range(slots)]
    place = (iota((LINE, width), 0) == iota((LINE, width), 1) // SPAN).astype(BF16)
    keep = iota((SPAN, width), 0) == iota((SPAN, width), 1) % SPAN
    row = iota((EXTRA, width), 0)
    for w in waits:
        w.wait()
    value = ends[2].astype(F32)
    value = jnp.where(row == TAIL_FIRST, ends[0].astype(F32)[0:1], value)
    value = jnp.where(row == TAIL_LAST, ends[1].astype(F32)[15:16], value)
    groups, rows, _ = lines.shape
    depth = rows // slots
    wide = lines[...].astype(F32)
    for s in range(slots):
        mine = [wide[g, s * depth : (s + 1) * depth] for g in range(groups)]
        spread = dot(jnp.concatenate(mine, axis=0).astype(BF16), place)
        own = jnp.sum(jnp.where(keep, spread, 0.0), axis=0, keepdims=True)
        value = jnp.where(row == PRIOR + s, own, value)
    held[drafts:, :] = value.astype(BF16)
    copies.start(held, small).wait()


def small_payload(draft, tail, mixes, got):
    slots, _, width = draft.shape
    size = (slots * DRAFT + EXTRA, width)
    return call(
        functools.partial(small_kernel, slots),
        (draft, tail, mixes, got),
        [HBM] * 4,
        [(size, BF16)],
        [
            pltpu.VMEM((3, 16, width), BF16),
            pltpu.VMEM((got.shape[0], got.shape[1], LINE), BF16),
            pltpu.VMEM(size, BF16),
            pltpu.SemaphoreType.DMA((5 + slots,)),
        ],
        "small_payload",
    )[0]


def head_ones(scale=1.0):
    r, c = iota((QUAD, QUAD), 0), iota((QUAD, QUAD), 1)
    return jnp.where(r // SPAN == c // SPAN, scale, 0.0).astype(BF16)


def head_masks(dtype):
    lane = iota((1, QUAD), 1) // SPAN
    return [(lane == h).astype(F32).astype(dtype) for h in range(QUAD // SPAN)]


def by_head(x, masks):
    return jnp.concatenate([x * m for m in masks], axis=0)


def own_rows(x, depth):
    lane = iota((depth, QUAD), 1) // SPAN
    out = x[:depth]
    for h in range(1, QUAD // SPAN):
        out = jnp.where(lane == h, x[h * depth : (h + 1) * depth], out)
    return out


def down_state(line, ones):
    keep = iota((SPAN, QUAD), 0) == iota((SPAN, QUAD), 1) % SPAN
    both = dot(split2(jnp.where(keep, line, 0.0), 0), ones)
    return both[:SPAN] + both[SPAN:]


def gathered(keys, v):
    return own_rows(dot_rows(keys.astype(BF16), v), SPAN)


def sums_after(n):
    t, u = iota((n, 2 * n), 0), iota((n, 2 * n), 1) & (n - 1)
    return (u > t).astype(BF16)


def mixed(x, previous, share):
    return (x + (previous - x) * share).astype(BF16)


def shares(rest):
    take = lambda n: rest[n : n + 1] + rest[n + 1 : n + 2] + rest[n + 2 : n + 3]
    return take(MIX_V), take(MIX_W)


def early_kernel(*refs):
    refs = list(refs)
    take = lambda n: [refs.pop(0) for _ in range(n)]
    xs_in, smalls_in = take(2), take(2)
    shrink_in, weights = take(2)
    v_out, w_out, xs, smalls, shrink, held, acc_v, acc_w, sems = take(9)
    width = xs.shape[2]
    me = lax.axis_index("tp")
    go = Copies(sems)
    waits = []
    for j in range(2):
        block = pl.ds(pl.multiple_of(jnp.bitwise_xor(me, j) * width, width), width)
        waits.append(
            [
                go.start(smalls_in[j], smalls.at[j]),
                go.start(xs_in[j], xs.at[j]),
                go.start(shrink_in.at[block, :], shrink.at[j]),
                go.start(weights.at[block, :], held.at[j]),
            ]
        )
    for j in range(2):
        for w in waits[j]:
            w.wait()
        x = xs[j].astype(F32)
        share_v, share_w = shares(smalls[j].astype(F32))
        previous = pltpu.roll(x, 1, 0)
        low = dot(mixed(x, previous, share_w), shrink[j])
        part = dot(mixed(x, previous, share_v), held[j])
        if j == 0:
            acc_w[...] = low
            acc_v[...] = part
        else:
            acc_w[...] += low
            acc_v[...] += part
    outs = [go.start(acc_v, v_out), go.start(acc_w, w_out)]
    for w in outs:
        w.wait()


def early(xs, smalls, shrink, weights):
    rows, width = xs[0].shape
    rank = shrink.shape[1]
    return call(
        early_kernel,
        (*xs, *smalls, shrink, weights),
        [HBM] * 6,
        [((rows, width), F32), ((rows, rank), F32)],
        [
            pltpu.VMEM((2, rows, width), BF16),
            pltpu.VMEM((2, *smalls[0].shape), BF16),
            pltpu.VMEM((2, width, rank), BF16),
            pltpu.VMEM((2, width, width), BF16),
            pltpu.VMEM((rows, width), F32),
            pltpu.VMEM((rows, rank), F32),
            pltpu.SemaphoreType.DMA((10,)),
        ],
        "early",
        4 * rows * width * width,
        4 * width * width,
    )


def final_kernel(slots, copies, direct, *refs):
    refs = list(refs)
    take = lambda n: [refs.pop(0) for _ in range(n)]
    owner, spans, admitted = take(3)
    xs_in, smalls_in = take(2), take(copies)
    part_v_in, part_w_in, shrink_in, expand_in, anchor_in, keys_in, draft_keys_in, got_in, weights = take(9)
    v_out, w_out, starts_out, back = take(4)
    xs, smalls, part_v, part_w, shrink, expand, anchor, keys, draft_keys, got, held = take(11)
    v_held, w_held, starts, sems = take(4)

    tail, width = xs.shape[1], xs.shape[2]
    rows = tail // PIECES
    quads = width // QUAD
    drafts = slots * DRAFT
    groups = got.shape[0]
    lines = SPAN // groups
    special = tail + drafts
    me = lax.axis_index("tp")
    blocks = [pl.ds(pl.multiple_of(jnp.bitwise_xor(me, j) * width, width), width) for j in range(copies)]
    go = Copies(sems)
    wait_got = go.start(got_in, got)
    wait_small = [go.start(smalls_in[j], smalls.at[j]) for j in range(copies)]
    wait_x = [go.start(xs_in[n], xs.at[n]) for n in range(2)]
    wait_shrink = go.start(shrink_in, shrink)
    wait_w = {j: go.start(weights.at[blocks[j], :], held.at[j]) for j in (2, 3, 0, 1)}
    wait_part = [go.start(part_v_in, part_v), go.start(part_w_in, part_w)]
    wait_part += [go.start(expand_in, expand), go.start(anchor_in, anchor)]
    wait_keys = [go.start(keys_in, keys), go.start(draft_keys_in, draft_keys)]
    first_slot = lax.axis_index("rep") * slots
    reqs = [owner[first_slot + s] for s in range(slots)]
    is_long = [spans[q] > DRAFT for q in reqs]
    counts = [admitted[q] for q in reqs]

    for w in wait_small:
        w.wait()

    def draft_mixes(j):
        d = smalls[j].astype(F32)
        rest = d[drafts:]
        share_v, share_w = shares(rest)
        row = iota(d.shape, 0)
        previous = pltpu.roll(d, 1, 0)
        for s in range(slots):
            own = rest[PRIOR + s : PRIOR + s + 1]
            first = jnp.where(is_long[s], rest[TAIL_LAST : TAIL_LAST + 1], own)
            previous = jnp.where(row == s * DRAFT, first, previous)
            if s == 0:
                previous = jnp.where(row == drafts + TAIL_FIRST, own, previous)
        return mixed(d, previous, share_v), mixed(d, previous, share_w), share_v, share_w

    wait_shrink.wait()
    acc_v = acc_w = None
    for n, j in enumerate((2, 3)):
        dv, dw, share_v, share_w = draft_mixes(j)
        wait_x[n].wait()
        x = xs[n].astype(F32)
        previous = pltpu.roll(x, 1, 0)
        xv = jnp.concatenate([mixed(x, previous, share_v), dv], axis=0)
        xw = jnp.concatenate([mixed(x, previous, share_w), dw], axis=0)
        low = dot(xw, shrink[blocks[j], :])
        wait_w[j].wait()
        part = dot(xv, held[j])
        acc_w = low if n == 0 else acc_w + low
        acc_v = part if n == 0 else acc_v + part
    draft_v, draft_w = acc_v[tail:], acc_w[tail:]
    for j in (0, 1):
        dv, dw, _, _ = draft_mixes(j)
        draft_w = draft_w + dot(dw, shrink[blocks[j], :])
        wait_w[j].wait()
        draft_v = draft_v + dot(dv, held[j])
    for w in wait_part:
        w.wait()
    v_held[0:tail, :] = (acc_v[:tail] + part_v[...]).astype(BF16)
    v_held[tail:, :] = draft_v.astype(BF16)
    low = jnp.concatenate([acc_w[:tail] + part_w[...], draft_w], axis=0)
    rate = -jnp.exp(anchor[...] + dot(jnp.tanh(low).astype(BF16), expand[...]))
    w_held[0:8, :] = jnp.where(iota((8, width), 0) == 0, 0.0, rate[:8])
    w_held[8:, :] = rate[8:]
    outs = [go.start(v_held, v_out), go.start(w_held, w_out)]
    for w in wait_keys:
        w.wait()
    wait_got.wait()

    ones = head_ones()
    after = sums_after(rows)
    masks = head_masks(F32)
    t, u = iota((drafts, 2 * drafts), 0), iota((drafts, 2 * drafts), 1) & (drafts - 1)
    limit = jnp.zeros(t.shape, jnp.int32)
    row, row_limit = iota((drafts, QUAD), 0), jnp.zeros((drafts, QUAD), jnp.int32)
    for s in range(slots):
        limit = jnp.where((t >= s * DRAFT) & (t < (s + 1) * DRAFT), s * DRAFT + counts[s], limit)
        row_limit = jnp.where(
            (row >= s * DRAFT) & (row < (s + 1) * DRAFT), s * DRAFT + counts[s], row_limit
        )
    draft_after = ((u > t) & (u < limit)).astype(BF16)
    taken = row < row_limit
    for p in range(quads):
        lanes = quad_lanes(p)
        parts, rest = [], jnp.zeros((1, QUAD), F32)
        for n in reversed(range(PIECES)):
            w = w_held[n * rows : (n + 1) * rows, lanes]
            k = keys[n * rows : (n + 1) * rows, lanes].astype(F32)
            k = k * jnp.exp(dot(after, split2(w, 0)) + rest)
            if n == 0:
                k = jnp.where(iota(k.shape, 0) == 0, 0.0, k)
            parts.append(k)
            rest = rest + jnp.sum(w, axis=0, keepdims=True)
        gained = gathered(jnp.concatenate(parts[::-1], axis=0), v_held[0:tail, lanes])
        begin = [
            jnp.concatenate(
                [got[g, :, lanes].astype(F32)[s * lines : (s + 1) * lines] for g in range(groups)], axis=0
            )
            for s in range(slots)
        ]
        starts[0, :, lanes] = begin[0].astype(BF16)
        lift = jnp.exp(down_state(w_held[special : special + 1, lanes], ones))
        key = down_state(keys[0:16, lanes].astype(F32)[0:1], ones)
        state = lift * begin[0] + key * v_held[special : special + 16, lanes].astype(F32)[0:1]
        starts[1, :, lanes] = state.astype(BF16)
        state = jnp.exp(down_state(rest, ones)) * state + gained
        begin[0] = jnp.where(is_long[0], state, begin[0])
        w = w_held[tail:special, lanes]
        k = draft_keys[:, lanes].astype(F32) * jnp.exp(dot(draft_after, split2(w, 0)))
        k = jnp.where(taken, k, 0.0)
        v = v_held[tail:special, lanes]
        closed = []
        for s in range(slots):
            starts[2 + s, :, lanes] = begin[s].astype(BF16)
            mine = slice(s * DRAFT, (s + 1) * DRAFT)
            upto = jnp.sum(jnp.where(taken[mine], w[mine], 0.0), axis=0, keepdims=True)
            closed.append(jnp.exp(down_state(upto, ones)) * begin[s] + gathered(k[mine], v[mine]))
        if direct:
            for g in range(groups):
                part = jnp.concatenate([c[g * lines : (g + 1) * lines] for c in closed], axis=0)
                back[g, :, lanes] = part.astype(BF16)
        else:
            for s in range(slots):
                back[s, :, lanes] = closed[s].astype(BF16)
    outs.append(go.start(starts, starts_out))

    tokens = smalls[0].astype(F32)
    row = iota(tokens.shape, 0)
    place = (iota((LINE, width), 0) == iota((LINE, width), 1) // SPAN).astype(BF16)
    keep = iota((SPAN, width), 0) == iota((SPAN, width), 1) % SPAN
    edges = []
    for s in range(slots):
        own = tokens[drafts + PRIOR + s : drafts + PRIOR + s + 1]
        first = jnp.where(is_long[s], tokens[drafts + TAIL_LAST : drafts + TAIL_LAST + 1], own)
        chosen = jnp.sum(
            jnp.where(row == s * DRAFT + counts[s] - 1, tokens, 0.0), axis=0, keepdims=True
        )
        edge = jnp.where(counts[s] > 0, chosen, first)
        edges.append(dot_lanes(jnp.where(keep, edge, 0.0).astype(BF16), place))
    if direct:
        for g in range(groups):
            part = jnp.concatenate([e[g * lines : (g + 1) * lines] for e in edges], axis=0)
            back[g, :, width:] = part.astype(BF16)
    else:
        for s in range(slots):
            back[s, :, width:] = edges[s].astype(BF16)
    for w in outs:
        w.wait()


def final(scalars, xs, smalls, part_v, part_w, maps, keys, draft_keys, got, weights, slots):
    copies = len(smalls)
    tail, width = xs[0].shape
    drafts = slots * DRAFT
    total = tail + drafts + EXTRA
    groups = got.shape[0]
    direct = SPAN // groups == 8
    back = (groups, got.shape[1]) if direct else (slots, SPAN)
    back = (*back, width + LINE)
    starts = (2 + slots, SPAN, width)
    args = [*scalars, *xs, *smalls, part_v, part_w, *maps, keys, draft_keys, got, weights]
    v, w, begins, ret = call(
        functools.partial(final_kernel, slots, copies, direct),
        args,
        [SMEM] * len(scalars) + [HBM] * (len(args) - len(scalars)),
        [((total, width), BF16), ((total, width), F32), (starts, BF16), (back, BF16)],
        [
            pltpu.VMEM((2, tail, width), BF16),
            pltpu.VMEM((copies, *smalls[0].shape), BF16),
            pltpu.VMEM(part_v.shape, F32),
            pltpu.VMEM(part_w.shape, F32),
            pltpu.VMEM(maps[0].shape, BF16),
            pltpu.VMEM(maps[1].shape, BF16),
            pltpu.VMEM((1, width), F32),
            pltpu.VMEM(keys.shape, BF16),
            pltpu.VMEM(draft_keys.shape, BF16),
            pltpu.VMEM(got.shape, BF16),
            pltpu.VMEM((copies, width, width), BF16),
            pltpu.VMEM((total, width), BF16),
            pltpu.VMEM((total, width), F32),
            pltpu.VMEM(starts, BF16),
            pltpu.SemaphoreType.DMA((32,)),
        ],
        "final",
        6 * tail * width * width,
        8 * width * width,
        [HBM, HBM, HBM, pl.BlockSpec(memory_space=pltpu.VMEM)],
    )
    if not direct:
        ret = ret.reshape(slots, groups, SPAN // groups, width + LINE).transpose(1, 0, 2, 3)
        ret = ret.reshape(groups, slots * SPAN // groups, width + LINE)
    return v, w, begins, ret


def levels_scores(r, k, rate, length, masks):
    n = r.shape[0]
    heads = len(masks)
    pieces = jnp.concatenate(split3(rate), axis=0)

    def level(n_level, total):
        half = lax.shift_left(jnp.int32(1), n_level)
        shift = n_level + 1
        t, u = iota((n, 3 * n), 0), iota((n, 3 * n), 1) % n
        edge = lax.shift_left(lax.shift_right_logical(t, shift), shift) + half
        after = (t >= edge) & (u >= edge) & (u < t)
        ahead = (t < edge) & (u > t) & (u < edge)
        decay = jnp.exp(dot((after | ahead).astype(BF16), pieces))
        row = iota(r.shape, 0)
        row_edge = lax.shift_left(lax.shift_right_logical(row, shift), shift) + half
        rt = jnp.where(row >= row_edge, r * decay, 0.0).astype(BF16)
        kt = jnp.where(row < row_edge, k * decay, 0.0)
        sc = dot_lanes(rt, by_head(kt, masks).astype(BF16))
        t2, s2 = iota((n, heads * n), 0), iota((n, heads * n), 1) & (n - 1)
        same = lax.shift_right_logical(t2, shift) == lax.shift_right_logical(s2, shift)
        return total + jnp.where(same, sc, 0.0)

    start = jnp.zeros((n, heads * n), F32)
    return lax.fori_loop(0, length.bit_length() - 1, level, start)


def answer(r, k, v, rate, boost, states, length, scaled, ones, masks):
    n = r.shape[0]
    count = n // length
    heads = len(masks)
    t, u = iota((n, 2 * n), 0), iota((n, 2 * n), 1) & (n - 1)
    t2, s2 = iota((n, heads * n), 0), iota((n, heads * n), 1) & (n - 1)
    earlier, keep = u < t, s2 < t2
    if count > 1:
        earlier = earlier & (u // length == t // length)
        keep = keep & (s2 // length == t2 // length)
    before = dot(earlier.astype(BF16), split2(rate, 0))
    if scaled:
        middle = [before[s * length + length // 2 :][:1] for s in range(count)]
        if count > 1:
            middle = [jnp.broadcast_to(m, (length, QUAD)) for m in middle]
            middle = jnp.concatenate(middle, axis=0)
        else:
            middle = middle[0]
        rt = (r * jnp.exp(before - middle)).astype(BF16)
        kt = k * jnp.exp(middle - before - rate)
        sc = jnp.where(keep, dot_lanes(rt, by_head(kt, masks).astype(BF16)), 0.0)
    else:
        sc = levels_scores(r, k, rate, length, masks)
    v32 = v.astype(F32)
    y = dot(sc.astype(BF16), by_head(v32, masks).astype(BF16))
    rs = (r * jnp.exp(before)).astype(BF16)
    outer = [
        dot(rs[s * length : (s + 1) * length], by_head(states[s], masks).astype(BF16))
        for s in range(count)
    ]
    y = y + (outer[0] if count == 1 else jnp.concatenate(outer, axis=0))
    return y + dot((r * k * boost).astype(BF16), ones) * v32


def normed(y, gain, bias, mean_ones):
    center = y - dot(y.astype(BF16), mean_ones)
    spread = dot((center * center).astype(BF16), mean_ones)
    return (center * lax.rsqrt(spread + EPS) * gain + bias).astype(BF16)


def outputs_kernel(slots, *refs):
    refs = list(refs)
    take = lambda n: [refs.pop(0) for _ in range(n)]
    owner, spans = take(2)
    v_in, w_in, r_in, k_in, rd_in, kd_in, starts_in = take(7)
    lines_in = take(3)
    tail_out, draft_out = take(2)
    v_held, w_held, r_held, k_held, rd, kd, starts, lines, states, out_held, draft_held, sems = take(12)
    tail, width = out_held.shape
    rows = tail // PIECES
    quads = width // QUAD
    drafts = slots * DRAFT
    special = tail + drafts
    go = Copies(sems)
    is_long = spans[owner[lax.axis_index("rep") * slots]] > DRAFT

    waits = [go.start(v_in, v_held), go.start(w_in, w_held), go.start(rd_in, rd), go.start(kd_in, kd)]
    waits += [go.start(starts_in, starts)]
    waits += [go.start(x, lines.at[n]) for n, x in enumerate(lines_in)]
    tails = [go.start(r_in, r_held), go.start(k_in, k_held)]
    ones, mean_ones = head_ones(), head_ones(1.0 / SPAN)
    masks = head_masks(F32)
    for w in waits:
        w.wait()

    def line(n, lanes):
        return lines[n, :, lanes]

    def draft_quad(p, scaled):
        lanes = quad_lanes(p)
        r, k = rd[:, lanes].astype(F32), kd[:, lanes].astype(F32)
        begin = [starts[2 + s, :, lanes].astype(F32) for s in range(slots)]
        y = answer(
            r, k, v_held[tail:special, lanes], w_held[tail:special, lanes], line(0, lanes),
            begin, DRAFT, scaled, ones, masks,
        )
        draft_held[:, lanes] = normed(y, line(1, lanes), line(2, lanes), mean_ones)

    sums = [
        jnp.sum(w_held[tail + s * DRAFT : tail + (s + 1) * DRAFT, :], axis=0, keepdims=True)
        for s in range(slots)
    ]
    safe = jnp.min(jnp.concatenate(sums, axis=0)) > SAFE

    @pl.when(safe)
    def _():
        for p in range(quads):
            draft_quad(p, True)

    @pl.when(jnp.logical_not(safe))
    def _():
        def body(p, carry):
            draft_quad(p, False)
            return carry

        lax.fori_loop(0, quads, body, 0)

    out_waits = [go.start(draft_held, draft_out)]
    for w in tails:
        w.wait()

    def tail_quad(n, p, scaled):
        lanes = quad_lanes(p)
        at = pl.ds(pl.multiple_of(n * rows, rows), rows)
        r, k = r_held[at, lanes].astype(F32), k_held[at, lanes].astype(F32)
        v, rate = v_held[at, lanes], w_held[at, lanes]
        first = (iota((rows, QUAD), 0) == 0) & (n == 0)
        state = states[:, lanes]
        zk = jnp.where(first, 0.0, k)
        y = answer(
            jnp.where(first, 0.0, r), zk, v, rate, line(0, lanes), [state], rows, scaled, ones, masks
        )
        r0, k0 = r[0:8], k[0:8]
        v0 = v_held[special : special + 16, lanes].astype(F32)[0:1]
        y0 = dot(r0.astype(BF16), by_head(starts[0, :, lanes].astype(F32), masks).astype(BF16))
        y0 = y0 + dot((r0 * k0 * line(0, lanes)).astype(BF16), ones) * v0
        y = jnp.where(first, y0[0:1], y)
        out_held[at, lanes] = normed(y, line(1, lanes), line(2, lanes), mean_ones)
        kept = jnp.exp(down_state(jnp.sum(rate, axis=0, keepdims=True), ones))
        gain = gathered(zk * jnp.exp(dot(sums_after(rows), split2(rate, 0))), v)
        states[:, lanes] = kept * state + gain

    @pl.when(is_long)
    def _():
        states[...] = starts[1].astype(F32)
        lowest = functools.reduce(
            jnp.minimum,
            [
                jnp.sum(w_held[n * rows : (n + 1) * rows, :], axis=0, keepdims=True)
                for n in range(PIECES)
            ],
        )
        fine = jnp.min(lowest) > SAFE

        @pl.when(fine)
        def _():
            def body(n, carry):
                for p in range(quads):
                    tail_quad(n, p, True)
                return carry

            lax.fori_loop(0, PIECES, body, 0)

        @pl.when(jnp.logical_not(fine))
        def _():
            def body(m, carry):
                tail_quad(m // quads, m % quads, False)
                return carry

            lax.fori_loop(0, PIECES * quads, body, 0)

    @pl.when(jnp.logical_not(is_long))
    def _():
        out_held[...] = jnp.zeros_like(out_held)

    out_waits.append(go.start(out_held, tail_out))
    for w in out_waits:
        w.wait()


def outputs(scalars, arrays, slots):
    v, w, r, k, rd, kd, starts = arrays[:7]
    tail, width = r.shape
    drafts = slots * DRAFT
    args = [*scalars, *arrays]
    return call(
        functools.partial(outputs_kernel, slots),
        args,
        [SMEM] * len(scalars) + [HBM] * (len(args) - len(scalars)),
        [((tail, width), BF16), ((drafts, width), BF16)],
        [
            pltpu.VMEM(v.shape, BF16),
            pltpu.VMEM(w.shape, F32),
            pltpu.VMEM(r.shape, BF16),
            pltpu.VMEM(k.shape, BF16),
            pltpu.VMEM(rd.shape, BF16),
            pltpu.VMEM(kd.shape, BF16),
            pltpu.VMEM(starts.shape, BF16),
            pltpu.VMEM((3, 1, width), F32),
            pltpu.VMEM((SPAN, width), F32),
            pltpu.VMEM((tail, width), BF16),
            pltpu.VMEM((drafts, width), BF16),
            pltpu.SemaphoreType.DMA((32,)),
        ],
        "outputs",
        16 * tail * width * LINE,
        16 * tail * width,
    )


def unpack_kernel(slots, owner, back, state_out, shift_out, held, sems):
    reqs, lines, width = state_out.shape
    heads = shift_out.shape[2]
    copy = pltpu.make_async_copy(back, held, sems.at[0])
    copy.start()
    copy.wait()
    for g in range(reqs // slots):
        rows = held[g].astype(F32)
        for s in range(slots):
            q = owner[g * slots + s]
            mine = rows[s * lines : (s + 1) * lines]
            state_out[q] = mine[:, :width]
            shift_out[q] = mine[:, width : width + heads].astype(BF16)


def unpack(lane_owner, back, slots, lines, width, heads):
    reqs = back.shape[0] * slots
    outs = [((reqs, lines, width), F32), ((reqs, lines, heads), BF16)]
    whole = lambda *shape: pl.BlockSpec(shape, lambda i: (0,) * len(shape))
    return pl.pallas_call(
        functools.partial(unpack_kernel, slots),
        grid=(1,),
        in_specs=[SMEM, HBM],
        out_specs=[whole(*s) for s, _ in outs],
        out_shape=[jax.ShapeDtypeStruct(s, t) for s, t in outs],
        scratch_shapes=[pltpu.VMEM(back.shape, BF16), pltpu.SemaphoreType.DMA((1,))],
        compiler_params=params(),
        name="unpack",
    )(lane_owner, back)


def local(
    groups,
    copies,
    suffix_source,
    suffix_accept,
    suffix_address,
    guess_lane_source,
    guess_lane_accept,
    guess_lane_address,
    content_map,
    forget_shrink_map,
    forget_expand_map,
    forget_lane_anchor,
    present_boost,
    content_blend_share,
    forget_blend_share,
    lane_normal_scale,
    lane_normal_shift,
    kernel_memory_saved,
    prior_source_saved,
    lane_owner,
    request_spans,
    admitted_guesses,
):
    width = content_map.shape[1]
    slots = guess_lane_source.shape[0]
    drafts = slots * DRAFT
    lines = kernel_memory_saved.shape[1]
    line = lambda x: x.reshape(1, width)

    def flip(x, k):
        return lax.ppermute(x, "tp", [(i, i ^ k) for i in range(copies)])

    tail = suffix_source[0]
    keys = suffix_address[0]
    draft_keys = guess_lane_address.reshape(drafts, width)
    cross, near = flip(tail, 2), flip(tail, 1)
    sent, mixes = pack(
        lane_owner,
        kernel_memory_saved,
        prior_source_saved,
        line(content_blend_share),
        line(forget_blend_share),
        groups,
    )
    got = lax.all_to_all(sent, "rep", 0, 0)
    part_v, part_w = early(
        [tail, near], [mixes, flip(mixes, 1)], forget_shrink_map, content_map
    )
    got, part_v, part_w = lax.optimization_barrier((got, part_v, part_w))
    small = small_payload(guess_lane_source, tail, mixes, got)
    small_cross = flip(small, 2)
    cross, small = lax.optimization_barrier((cross, small))
    far = flip(cross, 1)
    smalls = [small, flip(small, 1), small_cross, flip(small_cross, 1)]
    v, w, starts, ret = final(
        (lane_owner, request_spans, admitted_guesses),
        [cross, far],
        smalls,
        part_v,
        part_w,
        (forget_shrink_map, forget_expand_map, line(forget_lane_anchor)),
        keys,
        draft_keys,
        got,
        content_map,
        slots,
    )
    back = lax.all_to_all(ret, "rep", 0, 0)
    tail_out, draft_out = outputs(
        (lane_owner, request_spans),
        [
            v,
            w,
            suffix_accept[0],
            keys,
            guess_lane_accept.reshape(drafts, width),
            draft_keys,
            starts,
            line(present_boost),
            line(lane_normal_scale),
            line(lane_normal_shift),
        ],
        slots,
    )
    state_out, shift_out = unpack(lane_owner, back, slots, lines, width, width // SPAN)
    return (
        tail_out[None],
        draft_out.reshape(slots, DRAFT, width),
        state_out,
        shift_out,
    )


def solution(mesh):
    wide = P("rep", None, "tp")
    cached = P(None, "rep", "tp")
    placed = (wide,) * 6 + (P(None, "tp"), P(), P(None, "tp")) + (P("tp"),) * 6
    placed += (cached, cached, P(), P(), P())
    return jax.shard_map(
        functools.partial(local, mesh.shape["rep"], mesh.shape["tp"]),
        mesh=mesh,
        in_specs=placed,
        out_specs=(wide, wide, cached, cached),
        check_vma=False,
    )
```

```python
import functools

import jax
import jax.numpy as jnp
from jax import lax
from jax.experimental import pallas as pl
from jax.experimental.pallas import tpu as pltpu
from jax.sharding import PartitionSpec as P

SPAN = 64
DRAFT = 16
QUAD = 4 * SPAN
PIECES = 3
LINE = 128
EXTRA = 16
TAIL_FIRST, TAIL_LAST, MIX_V, MIX_W = 0, 1, 2, 5
EPS = 0.00064
SAFE = -60.0
F32, BF16 = jnp.float32, jnp.bfloat16
VMEM_MIB = 62
SMEM = pl.BlockSpec(memory_space=pltpu.SMEM)
HBM = pl.BlockSpec(memory_space=pltpu.HBM)


def params(mib=VMEM_MIB):
    return pltpu.CompilerParams(vmem_limit_bytes=mib * 1024 * 1024)


def iota(shape, dim):
    return lax.broadcasted_iota(jnp.int32, shape, dim)


def split2(x, axis):
    high = x.astype(BF16)
    return jnp.concatenate([high, (x - high.astype(F32)).astype(BF16)], axis=axis)


def split3(x):
    high = x.astype(BF16)
    rest = x - high.astype(F32)
    mid = rest.astype(BF16)
    return high, mid, (rest - mid.astype(F32)).astype(BF16)


def dot(a, b):
    return jnp.dot(a, b, preferred_element_type=F32)


def dot_rows(a, b):
    return lax.dot_general(a, b, (((0,), (0,)), ((), ())), preferred_element_type=F32)


def dot_lanes(a, b):
    return lax.dot_general(a, b, (((1,), (1,)), ((), ())), preferred_element_type=F32)


def quad_lanes(p):
    if isinstance(p, int):
        return slice(p * QUAD, (p + 1) * QUAD)
    return pl.ds(pl.multiple_of(p * QUAD, QUAD), QUAD)


class Copies:
    def __init__(self, sems):
        self.sems, self.used = sems, 0

    def start(self, source, target):
        copy = pltpu.make_async_copy(source, target, self.sems.at[self.used])
        self.used += 1
        copy.start()
        return copy


def call(kernel, args, in_specs, outs, scratch, name, flops=0, moved=0, out_specs=None):
    return pl.pallas_call(
        kernel,
        in_specs=in_specs,
        out_specs=out_specs or [HBM] * len(outs),
        out_shape=[jax.ShapeDtypeStruct(s, t) for s, t in outs],
        scratch_shapes=scratch,
        compiler_params=params(),
        cost_estimate=pl.CostEstimate(flops=flops, bytes_accessed=moved, transcendentals=0),
        name=name,
    )(*args)


def pack_kernel(slots, owner, state, prior, out, held, cached, lines, sems):
    groups, rows, _ = out.shape
    width = state.shape[2]
    heads = prior.shape[2]
    go = Copies(sems)
    second = go.start(state, held)
    first = go.start(prior, cached)
    lines[...] = jnp.zeros_like(lines)
    first.wait()
    lines[:, :, 0:heads] = cached[...].astype(F32)
    second.wait()
    for g in range(groups):
        reqs = [owner[g * slots + s] for s in range(slots)]
        out[g, :, 0:width] = jnp.concatenate([held[q] for q in reqs], axis=0).astype(BF16)
        out[g, :, width:] = jnp.concatenate([lines[q] for q in reqs], axis=0).astype(BF16)


def pack(lane_owner, state, prior, groups):
    reqs, depth, width = state.shape
    slots = reqs // groups
    out = (groups, slots * depth, width + LINE)
    return pl.pallas_call(
        functools.partial(pack_kernel, slots),
        grid=(1,),
        in_specs=[SMEM, HBM, HBM],
        out_specs=pl.BlockSpec(out, lambda i: (0, 0, 0)),
        out_shape=jax.ShapeDtypeStruct(out, BF16),
        scratch_shapes=[
            pltpu.VMEM(state.shape, F32),
            pltpu.VMEM(prior.shape, BF16),
            pltpu.VMEM((reqs, depth, LINE), F32),
            pltpu.SemaphoreType.DMA((2,)),
        ],
        compiler_params=params(),
        name="pack",
    )(lane_owner, state, prior)


def small_kernel(slots, draft, tail, mix_v, mix_w, small, ends, shares, held, sems):
    copies = Copies(sems)
    last = tail.shape[0] - 16
    drafts = slots * DRAFT
    width = held.shape[1]
    waits = [
        copies.start(tail.at[pl.ds(0, 16), :], ends.at[0]),
        copies.start(tail.at[pl.ds(last, 16), :], ends.at[1]),
        copies.start(mix_v, shares.at[0]),
        copies.start(mix_w, shares.at[1]),
    ]
    waits += [copies.start(draft.at[s], held.at[pl.ds(s * DRAFT, DRAFT), :]) for s in range(slots)]
    row = iota((EXTRA, width), 0)
    for w in waits:
        w.wait()
    value = jnp.where(row == TAIL_FIRST, ends[0].astype(F32)[0:1], 0.0)
    value = jnp.where(row == TAIL_LAST, ends[1].astype(F32)[15:16], value)
    for n, base in enumerate((MIX_V, MIX_W)):
        for m, part in enumerate(split3(shares[n])):
            value = jnp.where(row == base + m, part.astype(F32), value)
    held[drafts:, :] = value.astype(BF16)
    copies.start(held, small).wait()


def small_payload(draft, tail, mix_v, mix_w):
    slots, _, width = draft.shape
    size = (slots * DRAFT + EXTRA, width)
    return call(
        functools.partial(small_kernel, slots),
        (draft, tail, mix_v, mix_w),
        [HBM] * 4,
        [(size, BF16)],
        [
            pltpu.VMEM((2, 16, width), BF16),
            pltpu.VMEM((2, 1, width), F32),
            pltpu.VMEM(size, BF16),
            pltpu.SemaphoreType.DMA((5 + slots,)),
        ],
        "small_payload",
    )[0]


def head_ones(scale=1.0):
    r, c = iota((QUAD, QUAD), 0), iota((QUAD, QUAD), 1)
    return jnp.where(r // SPAN == c // SPAN, scale, 0.0).astype(BF16)


def head_masks(dtype):
    lane = iota((1, QUAD), 1) // SPAN
    return [(lane == h).astype(F32).astype(dtype) for h in range(QUAD // SPAN)]


def by_head(x, masks):
    return jnp.concatenate([x * m for m in masks], axis=0)


def own_rows(x, depth):
    lane = iota((depth, QUAD), 1) // SPAN
    out = x[:depth]
    for h in range(1, QUAD // SPAN):
        out = jnp.where(lane == h, x[h * depth : (h + 1) * depth], out)
    return out


def down_state(line, ones):
    keep = iota((SPAN, QUAD), 0) == iota((SPAN, QUAD), 1) % SPAN
    both = dot(split2(jnp.where(keep, line, 0.0), 0), ones)
    return both[:SPAN] + both[SPAN:]


def gathered(keys, v):
    return own_rows(dot_rows(keys.astype(BF16), v), SPAN)


def sums_after(n):
    t, u = iota((n, 2 * n), 0), iota((n, 2 * n), 1) & (n - 1)
    return (u > t).astype(BF16)


def mixed(x, previous, share):
    return (x + (previous - x) * share).astype(BF16)


def shares_of(rest):
    take = lambda n: rest[n : n + 1] + rest[n + 1 : n + 2] + rest[n + 2 : n + 3]
    return take(MIX_V), take(MIX_W)


def draft_mixes(d, owns, is_long, slots):
    drafts = slots * DRAFT
    rest = d[drafts:]
    share_v, share_w = shares_of(rest)
    row = iota(d.shape, 0)
    previous = pltpu.roll(d, 1, 0)
    for s in range(slots):
        own = owns[s : s + 1]
        first = jnp.where(is_long[s], rest[TAIL_LAST : TAIL_LAST + 1], own)
        previous = jnp.where(row == s * DRAFT, first, previous)
        if s == 0:
            previous = jnp.where(row == drafts + TAIL_FIRST, own, previous)
    return mixed(d, previous, share_v), mixed(d, previous, share_w), share_v, share_w


def long_slots(owner, spans, slots):
    first = lax.axis_index("rep") * slots
    return [spans[owner[first + s]] > DRAFT for s in range(slots)]


def feature_block(j, width):
    return pl.ds(pl.multiple_of(jnp.bitwise_xor(lax.axis_index("tp"), j) * width, width), width)


def early_kernel(*refs):
    refs = list(refs)
    take = lambda n: [refs.pop(0) for _ in range(n)]
    xs_in, shares_in = take(2), take(4)
    shrink_in, weights = take(2)
    v_out, w_out, xs, shares, shrink, held, acc_v, acc_w, sems = take(9)
    width = xs.shape[2]
    go = Copies(sems)
    waits = []
    for j in range(2):
        block = feature_block(j, width)
        waits.append(
            [
                go.start(shares_in[2 * j], shares.at[2 * j]),
                go.start(shares_in[2 * j + 1], shares.at[2 * j + 1]),
                go.start(xs_in[j], xs.at[j]),
                go.start(shrink_in.at[block, :], shrink.at[j]),
                go.start(weights.at[block, :], held.at[j]),
            ]
        )
    for j in range(2):
        for w in waits[j]:
            w.wait()
        x = xs[j].astype(F32)
        previous = pltpu.roll(x, 1, 0)
        low = dot(mixed(x, previous, shares[2 * j + 1]), shrink[j])
        part = dot(mixed(x, previous, shares[2 * j]), held[j])
        if j == 0:
            acc_w[...] = low
            acc_v[...] = part
        else:
            acc_w[...] += low
            acc_v[...] += part
    outs = [go.start(acc_v, v_out), go.start(acc_w, w_out)]
    for w in outs:
        w.wait()


def early(xs, shares, shrink, weights):
    rows, width = xs[0].shape
    rank = shrink.shape[1]
    return call(
        early_kernel,
        (*xs, *shares, shrink, weights),
        [HBM] * 8,
        [((rows, width), F32), ((rows, rank), F32)],
        [
            pltpu.VMEM((2, rows, width), BF16),
            pltpu.VMEM((4, 1, width), F32),
            pltpu.VMEM((2, width, rank), BF16),
            pltpu.VMEM((2, width, width), BF16),
            pltpu.VMEM((rows, width), F32),
            pltpu.VMEM((rows, rank), F32),
            pltpu.SemaphoreType.DMA((12,)),
        ],
        "early",
        4 * rows * width * width,
        4 * width * width,
    )


def owns_kernel(slots, got_in, out, lines, held, sems):
    width = out.shape[1]
    copy = pltpu.make_async_copy(got_in.at[:, :, pl.ds(width, LINE)], lines, sems.at[0])
    copy.start()
    place = (iota((LINE, width), 0) == iota((LINE, width), 1) // SPAN).astype(BF16)
    keep = iota((SPAN, width), 0) == iota((SPAN, width), 1) % SPAN
    row = iota((EXTRA, width), 0)
    groups, per, _ = lines.shape
    depth = per // slots
    copy.wait()
    wide = lines[...].astype(F32)
    value = jnp.zeros((EXTRA, width), F32)
    for s in range(slots):
        mine = [wide[g, s * depth : (s + 1) * depth] for g in range(groups)]
        spread = dot(jnp.concatenate(mine, axis=0).astype(BF16), place)
        own = jnp.sum(jnp.where(keep, spread, 0.0), axis=0, keepdims=True)
        value = jnp.where(row == s, own, value)
    held[...] = value.astype(BF16)
    copy = pltpu.make_async_copy(held, out, sems.at[1])
    copy.start()
    copy.wait()


def own_inputs(got, slots, width):
    return call(
        functools.partial(owns_kernel, slots),
        (got,),
        [HBM],
        [((EXTRA, width), BF16)],
        [
            pltpu.VMEM((got.shape[0], got.shape[1], LINE), BF16),
            pltpu.VMEM((EXTRA, width), BF16),
            pltpu.SemaphoreType.DMA((2,)),
        ],
        "own_inputs",
    )[0]


def final_kernel(slots, copies, direct, *refs):
    refs = list(refs)
    take = lambda n: [refs.pop(0) for _ in range(n)]
    owner, spans, admitted = take(3)
    xs_in, smalls_in, owns_in, parts_in = take(2), take(copies), take(copies), take(2)
    shrink_in, expand_in, anchor_in, keys_in, draft_keys_in, got_in, weights = take(7)
    v_out, low_out, starts_out, back = take(4)
    xs, smalls, owns, part_v, part_w, shrink, expand, anchor, keys, draft_keys, got, held = take(12)
    v_held, w_held, low_held, starts, sems = take(5)

    tail, width = xs.shape[1:]
    rows = tail // PIECES
    quads = width // QUAD
    drafts = slots * DRAFT
    groups = got.shape[0]
    lines = SPAN // groups
    special = tail + drafts
    go = Copies(sems)
    blocks = [feature_block(j, width) for j in range(copies)]
    wait_small = [go.start(smalls_in[j], smalls.at[j]) for j in range(copies)]
    wait_small += [go.start(owns_in[j], owns.at[j]) for j in range(copies)]
    wait_x, wait_w = [], {}
    for n in range(2):
        wait_x.append(go.start(xs_in[n], xs.at[n]))
        if n == 0:
            wait_shrink = go.start(shrink_in, shrink)
        wait_w[2 + n] = go.start(weights.at[blocks[2 + n], :], held.at[2 + n])
    for j in range(2):
        wait_w[j] = go.start(weights.at[blocks[j], :], held.at[j])
    wait_part = [go.start(parts_in[0], part_v), go.start(parts_in[1], part_w)]
    wait_part += [go.start(expand_in, expand), go.start(anchor_in, anchor)]
    wait_keys = [go.start(keys_in, keys), go.start(draft_keys_in, draft_keys), go.start(got_in, got)]
    is_long = long_slots(owner, spans, slots)
    first_slot = lax.axis_index("rep") * slots
    counts = [admitted[owner[first_slot + s]] for s in range(slots)]

    for w in wait_small:
        w.wait()

    def drafts_of(j):
        return draft_mixes(smalls[j].astype(F32), owns[j].astype(F32), is_long, slots)

    acc_v = acc_w = None
    for n in range(2):
        dv, dw, share_v, share_w = drafts_of(2 + n)
        wait_x[n].wait()
        now = xs[n].astype(F32)
        previous = pltpu.roll(now, 1, 0)
        xv = jnp.concatenate([mixed(now, previous, share_v), dv], axis=0)
        xw = jnp.concatenate([mixed(now, previous, share_w), dw], axis=0)
        if n == 0:
            wait_shrink.wait()
        low = dot(xw, shrink[blocks[2 + n], :])
        wait_w[2 + n].wait()
        part = dot(xv, held[2 + n])
        acc_w = low if n == 0 else acc_w + low
        acc_v = part if n == 0 else acc_v + part
    draft_v, draft_w = acc_v[tail:], acc_w[tail:]
    for j in range(2):
        dv, dw, _, _ = drafts_of(j)
        draft_w = draft_w + dot(dw, shrink[blocks[j], :])
        wait_w[j].wait()
        draft_v = draft_v + dot(dv, held[j])
    for w in wait_part:
        w.wait()
    v_held[0:tail, :] = (acc_v[:tail] + part_v[...]).astype(BF16)
    v_held[tail:, :] = draft_v.astype(BF16)
    acc_w = jnp.concatenate([acc_w[:tail] + part_w[...], draft_w], axis=0)
    low_held[...] = jnp.tanh(acc_w).astype(BF16)
    rate = -jnp.exp(anchor[...] + dot(low_held[...], expand[...]))
    w_held[0:8, :] = jnp.where(iota((8, width), 0) == 0, 0.0, rate[:8])
    w_held[8:, :] = rate[8:]
    outs = [go.start(v_held, v_out), go.start(low_held, low_out)]
    for w in wait_keys:
        w.wait()

    ones = head_ones()
    after = sums_after(rows)
    t, u = iota((drafts, 2 * drafts), 0), iota((drafts, 2 * drafts), 1) & (drafts - 1)
    limit = jnp.zeros(t.shape, jnp.int32)
    row, row_limit = iota((drafts, QUAD), 0), jnp.zeros((drafts, QUAD), jnp.int32)
    for s in range(slots):
        limit = jnp.where((t >= s * DRAFT) & (t < (s + 1) * DRAFT), s * DRAFT + counts[s], limit)
        row_limit = jnp.where(
            (row >= s * DRAFT) & (row < (s + 1) * DRAFT), s * DRAFT + counts[s], row_limit
        )
    draft_after = ((u > t) & (u < limit)).astype(BF16)
    taken = row < row_limit
    for p in range(quads):
        lanes = quad_lanes(p)
        parts, rest = [], jnp.zeros((1, QUAD), F32)
        for n in reversed(range(PIECES)):
            w = w_held[n * rows : (n + 1) * rows, lanes]
            k = keys[n * rows : (n + 1) * rows, lanes].astype(F32)
            k = k * jnp.exp(dot(after, split2(w, 0)) + rest)
            if n == 0:
                k = jnp.where(iota(k.shape, 0) == 0, 0.0, k)
            parts.append(k)
            rest = rest + jnp.sum(w, axis=0, keepdims=True)
        gained = gathered(jnp.concatenate(parts[::-1], axis=0), v_held[0:tail, lanes])
        begin = [
            jnp.concatenate(
                [got[g, :, lanes].astype(F32)[s * lines : (s + 1) * lines] for g in range(groups)], axis=0
            )
            for s in range(slots)
        ]
        starts[0, :, lanes] = begin[0].astype(BF16)
        lift = jnp.exp(down_state(w_held[special : special + 1, lanes], ones))
        key = down_state(keys[0:16, lanes].astype(F32)[0:1], ones)
        state = lift * begin[0] + key * v_held[special : special + 16, lanes].astype(F32)[0:1]
        starts[1, :, lanes] = state.astype(BF16)
        state = jnp.exp(down_state(rest, ones)) * state + gained
        begin[0] = jnp.where(is_long[0], state, begin[0])
        w = w_held[tail:special, lanes]
        k = draft_keys[:, lanes].astype(F32) * jnp.exp(dot(draft_after, split2(w, 0)))
        k = jnp.where(taken, k, 0.0)
        v = v_held[tail:special, lanes]
        closed = []
        for s in range(slots):
            starts[2 + s, :, lanes] = begin[s].astype(BF16)
            mine = slice(s * DRAFT, (s + 1) * DRAFT)
            upto = jnp.sum(jnp.where(taken[mine], w[mine], 0.0), axis=0, keepdims=True)
            closed.append(jnp.exp(down_state(upto, ones)) * begin[s] + gathered(k[mine], v[mine]))
        if direct:
            for g in range(groups):
                part = jnp.concatenate([c[g * lines : (g + 1) * lines] for c in closed], axis=0)
                back[g, :, lanes] = part.astype(BF16)
        else:
            for s in range(slots):
                back[s, :, lanes] = closed[s].astype(BF16)
    outs.append(go.start(starts, starts_out))

    tokens = smalls[0].astype(F32)
    row = iota(tokens.shape, 0)
    place = (iota((LINE, width), 0) == iota((LINE, width), 1) // SPAN).astype(BF16)
    keep = iota((SPAN, width), 0) == iota((SPAN, width), 1) % SPAN
    edges = []
    for s in range(slots):
        own = owns[0].astype(F32)[s : s + 1]
        first = jnp.where(is_long[s], tokens[drafts + TAIL_LAST : drafts + TAIL_LAST + 1], own)
        chosen = jnp.sum(
            jnp.where(row == s * DRAFT + counts[s] - 1, tokens, 0.0), axis=0, keepdims=True
        )
        edge = jnp.where(counts[s] > 0, chosen, first)
        edges.append(dot_lanes(jnp.where(keep, edge, 0.0).astype(BF16), place))
    if direct:
        for g in range(groups):
            part = jnp.concatenate([e[g * lines : (g + 1) * lines] for e in edges], axis=0)
            back[g, :, width:] = part.astype(BF16)
    else:
        for s in range(slots):
            back[s, :, width:] = edges[s].astype(BF16)
    for w in outs:
        w.wait()


def final(scalars, xs, smalls, owns, parts, maps, keys, draft_keys, got, weights, slots):
    tail, width = xs[0].shape
    total = tail + smalls[0].shape[0]
    copies = len(smalls)
    groups = got.shape[0]
    rank = maps[0].shape[1]
    direct = SPAN // groups == 8
    back = (groups, got.shape[1]) if direct else (slots, SPAN)
    back = (*back, width + LINE)
    starts = (2 + slots, SPAN, width)
    args = [*scalars, *xs, *smalls, *owns, *parts, *maps, keys, draft_keys, got, weights]
    v, low, begins, ret = call(
        functools.partial(final_kernel, slots, copies, direct),
        args,
        [SMEM] * len(scalars) + [HBM] * (len(args) - len(scalars)),
        [((total, width), BF16), ((total, rank), BF16), (starts, BF16), (back, BF16)],
        [
            pltpu.VMEM((2, tail, width), BF16),
            pltpu.VMEM((copies, *smalls[0].shape), BF16),
            pltpu.VMEM((copies, *owns[0].shape), BF16),
            pltpu.VMEM((tail, width), F32),
            pltpu.VMEM((tail, rank), F32),
            pltpu.VMEM(maps[0].shape, BF16),
            pltpu.VMEM(maps[1].shape, BF16),
            pltpu.VMEM((1, width), F32),
            pltpu.VMEM(keys.shape, BF16),
            pltpu.VMEM(draft_keys.shape, BF16),
            pltpu.VMEM(got.shape, BF16),
            pltpu.VMEM((copies, width, width), BF16),
            pltpu.VMEM((total, width), BF16),
            pltpu.VMEM((total, width), F32),
            pltpu.VMEM((total, rank), BF16),
            pltpu.VMEM(starts, BF16),
            pltpu.SemaphoreType.DMA((32,)),
        ],
        "final",
        4 * tail * width * width,
        4 * width * width,
        [HBM, HBM, HBM, pl.BlockSpec(memory_space=pltpu.VMEM)],
    )
    if not direct:
        ret = ret.reshape(slots, groups, SPAN // groups, width + LINE).transpose(1, 0, 2, 3)
        ret = ret.reshape(groups, slots * SPAN // groups, width + LINE)
    return v, low, begins, ret


def levels_scores(r, k, rate, length, masks):
    n = r.shape[0]
    heads = len(masks)
    pieces = jnp.concatenate(split3(rate), axis=0)

    def level(n_level, total):
        half = lax.shift_left(jnp.int32(1), n_level)
        shift = n_level + 1
        t, u = iota((n, 3 * n), 0), iota((n, 3 * n), 1) % n
        edge = lax.shift_left(lax.shift_right_logical(t, shift), shift) + half
        after = (t >= edge) & (u >= edge) & (u < t)
        ahead = (t < edge) & (u > t) & (u < edge)
        decay = jnp.exp(dot((after | ahead).astype(BF16), pieces))
        row = iota(r.shape, 0)
        row_edge = lax.shift_left(lax.shift_right_logical(row, shift), shift) + half
        rt = jnp.where(row >= row_edge, r * decay, 0.0).astype(BF16)
        kt = jnp.where(row < row_edge, k * decay, 0.0)
        sc = dot_lanes(rt, by_head(kt, masks).astype(BF16))
        t2, s2 = iota((n, heads * n), 0), iota((n, heads * n), 1) & (n - 1)
        same = lax.shift_right_logical(t2, shift) == lax.shift_right_logical(s2, shift)
        return total + jnp.where(same, sc, 0.0)

    start = jnp.zeros((n, heads * n), F32)
    return lax.fori_loop(0, length.bit_length() - 1, level, start)


def answers(r, k, v, rate, boost, states, length, scaled, ones, masks):
    n = r[0].shape[0]
    count = n // length
    heads = len(masks)
    every = range(len(r))
    t, u = iota((n, 2 * n), 0), iota((n, 2 * n), 1) & (n - 1)
    t2, s2 = iota((n, heads * n), 0), iota((n, heads * n), 1) & (n - 1)
    earlier, keep = u < t, s2 < t2
    if count > 1:
        earlier = earlier & (u // length == t // length)
        keep = keep & (s2 // length == t2 // length)
    earlier = earlier.astype(BF16)
    before = [dot(earlier, split2(x, 0)) for x in rate]
    if scaled:
        middle = []
        for x in before:
            rows = [x[s * length + length // 2 :][:1] for s in range(count)]
            if count > 1:
                rows = [jnp.concatenate([jnp.broadcast_to(m, (length, QUAD)) for m in rows], axis=0)]
            middle.append(rows[0])
        rt = [(r[i] * jnp.exp(before[i] - middle[i])).astype(BF16) for i in every]
        kt = [(k[i] * jnp.exp(middle[i] - before[i] - rate[i])).astype(BF16) for i in every]
        sc = [dot_lanes(rt[i], by_head(kt[i], masks)) for i in every]
        sc = [jnp.where(keep, x, 0.0).astype(BF16) for x in sc]
    else:
        sc = [levels_scores(r[i], k[i], rate[i], length, masks).astype(BF16) for i in every]
    bonus = [dot((r[i] * k[i] * boost[i]).astype(BF16), ones) * v[i].astype(F32) for i in every]
    rs = [(r[i] * jnp.exp(before[i])).astype(BF16) for i in every]
    y = [dot(sc[i], by_head(v[i], masks)) + bonus[i] for i in every]
    for i in every:
        outer = [
            dot(rs[i][s * length : (s + 1) * length], by_head(states[i][s], masks))
            for s in range(count)
        ]
        y[i] = y[i] + (outer[0] if count == 1 else jnp.concatenate(outer, axis=0))
    return y


def normed(y, gain, bias, mean_ones):
    every = range(len(y))
    center = [x - dot(x.astype(BF16), mean_ones) for x in y]
    spread = [dot((x * x).astype(BF16), mean_ones) for x in center]
    return [
        (center[i] * lax.rsqrt(spread[i] + EPS) * gain[i] + bias[i]).astype(BF16) for i in every
    ]


def outputs_kernel(slots, *refs):
    refs = list(refs)
    take = lambda n: [refs.pop(0) for _ in range(n)]
    owner, spans = take(2)
    v_in, low_in, expand_in, anchor_in, r_in, k_in, rd_in, kd_in, starts_in = take(9)
    lines_in = take(3)
    tail_out, draft_out = take(2)
    low, expand, anchor, v_held, w_held, r_held, k_held, rd, kd, starts, lines, states, out_held, draft_held, sems, done = take(16)
    tail, width = out_held.shape
    rows = tail // PIECES
    quads = width // QUAD
    drafts = slots * DRAFT
    special = tail + drafts
    go = Copies(sems)
    is_long = spans[owner[lax.axis_index("rep") * slots]] > DRAFT

    def leaving(n):
        at = pl.ds(n * rows, rows)
        return pltpu.make_async_copy(out_held.at[at, :], tail_out.at[at, :], done.at[n])

    def send(n):
        leaving(n).start()

    late = pl.ds(tail, drafts + EXTRA)
    wait_rate = [go.start(low_in, low), go.start(expand_in, expand), go.start(anchor_in, anchor)]
    waits = [go.start(v_in.at[late, :], v_held.at[late, :])]
    waits += [go.start(rd_in, rd), go.start(kd_in, kd), go.start(starts_in, starts)]
    waits += [go.start(x, lines.at[n]) for n, x in enumerate(lines_in)]
    pieces = [pl.ds(n * rows, rows) for n in range(PIECES)]
    loads = []
    for at in pieces:
        loads.append(
            [
                go.start(r_in.at[at, :], r_held.at[at, :]),
                go.start(k_in.at[at, :], k_held.at[at, :]),
                go.start(v_in.at[at, :], v_held.at[at, :]),
            ]
        )
    ones, mean_ones = head_ones(), head_ones(1.0 / SPAN)
    masks = head_masks(BF16)
    for w in wait_rate:
        w.wait()
    rate = -jnp.exp(anchor[...] + dot(low[...], expand[...]))
    w_held[0:8, :] = jnp.where(iota((8, width), 0) == 0, 0.0, rate[:8])
    w_held[8:, :] = rate[8:]
    for w in waits:
        w.wait()

    def line(n, lanes):
        return lines[n, :, lanes]

    def draft_quads(which, scaled):
        lanes = [quad_lanes(p) for p in which]
        y = answers(
            [rd[:, at].astype(F32) for at in lanes],
            [kd[:, at].astype(F32) for at in lanes],
            [v_held[tail:special, at] for at in lanes],
            [w_held[tail:special, at] for at in lanes],
            [line(0, at) for at in lanes],
            [[starts[2 + s, :, at] for s in range(slots)] for at in lanes],
            DRAFT, scaled, ones, masks,
        )
        out = normed(y, [line(1, at) for at in lanes], [line(2, at) for at in lanes], mean_ones)
        for at, x in zip(lanes, out):
            draft_held[:, at] = x

    sums = [
        jnp.sum(w_held[tail + s * DRAFT : tail + (s + 1) * DRAFT, :], axis=0, keepdims=True)
        for s in range(slots)
    ]
    safe = jnp.min(jnp.concatenate(sums, axis=0)) > SAFE

    @pl.when(safe)
    def _():
        draft_quads(range(quads), True)

    @pl.when(jnp.logical_not(safe))
    def _():
        def body(p, carry):
            draft_quads([p], False)
            return carry

        lax.fori_loop(0, quads, body, 0)

    out_waits = [go.start(draft_held, draft_out)]

    def tail_quads(n, which, scaled, carry_on):
        lanes = [quad_lanes(p) for p in which]
        every = range(len(lanes))
        at = pieces[n] if isinstance(n, int) else pl.ds(pl.multiple_of(n * rows, rows), rows)
        r = [r_held[at, x].astype(F32) for x in lanes]
        k = [k_held[at, x].astype(F32) for x in lanes]
        v = [v_held[at, x] for x in lanes]
        rate = [w_held[at, x] for x in lanes]
        state = [states[:, x] for x in lanes]
        boost = [line(0, x) for x in lanes]
        zr, zk = r, k
        if not isinstance(n, int) or n == 0:
            first = (iota((rows, QUAD), 0) == 0) & (n == 0)
            zr, zk = [jnp.where(first, 0.0, x) for x in r], [jnp.where(first, 0.0, x) for x in k]
        y = answers(
            zr, zk, v, rate, boost, [[x.astype(BF16)] for x in state], rows, scaled, ones, masks
        )
        if not isinstance(n, int) or n == 0:
            for i in every:
                r0, k0 = r[i][0:8], k[i][0:8]
                v0 = v_held[special : special + EXTRA, lanes[i]].astype(F32)[0:1]
                y0 = dot(r0.astype(BF16), by_head(starts[0, :, lanes[i]], masks))
                y0 = y0 + dot((r0 * k0 * boost[i]).astype(BF16), ones) * v0
                y[i] = jnp.where(first, y0[0:1], y[i])
        out = normed(y, [line(1, x) for x in lanes], [line(2, x) for x in lanes], mean_ones)
        for i in every:
            out_held[at, lanes[i]] = out[i]
        if carry_on:
            after = sums_after(rows)
            kept = [down_state(jnp.sum(x, axis=0, keepdims=True), ones) for x in rate]
            late = [dot(after, split2(x, 0)) for x in rate]
            gain = [gathered(zk[i] * jnp.exp(late[i]), v[i]) for i in every]
            for i in every:
                states[:, lanes[i]] = jnp.exp(kept[i]) * state[i] + gain[i]

    @pl.when(is_long)
    def _():
        states[...] = starts[1].astype(F32)
        lowest = functools.reduce(
            jnp.minimum,
            [
                jnp.sum(w_held[n * rows : (n + 1) * rows, :], axis=0, keepdims=True)
                for n in range(PIECES)
            ],
        )
        fine = jnp.min(lowest) > SAFE

        @pl.when(fine)
        def _():
            for n in range(PIECES):
                for w in loads[n]:
                    w.wait()
                tail_quads(n, range(quads), True, n < PIECES - 1)
                send(n)

        @pl.when(jnp.logical_not(fine))
        def _():
            for group in loads:
                for w in group:
                    w.wait()

            def body(m, carry):
                tail_quads(m // quads, [m % quads], False, True)
                return carry

            lax.fori_loop(0, PIECES * quads, body, 0)
            for n in range(PIECES):
                send(n)

    @pl.when(jnp.logical_not(is_long))
    def _():
        for group in loads:
            for w in group:
                w.wait()
        out_held[...] = jnp.zeros_like(out_held)
        for n in range(PIECES):
            send(n)

    for w in out_waits:
        w.wait()
    for n in range(PIECES):
        leaving(n).wait()


def outputs(scalars, arrays, slots):
    v, low, expand, anchor, r, k, rd, kd, starts = arrays[:9]
    tail, width = r.shape
    drafts = slots * DRAFT
    args = [*scalars, *arrays]
    return call(
        functools.partial(outputs_kernel, slots),
        args,
        [SMEM] * len(scalars) + [HBM] * (len(args) - len(scalars)),
        [((tail, width), BF16), ((drafts, width), BF16)],
        [
            pltpu.VMEM(low.shape, BF16),
            pltpu.VMEM(expand.shape, BF16),
            pltpu.VMEM(anchor.shape, F32),
            pltpu.VMEM(v.shape, BF16),
            pltpu.VMEM(v.shape, F32),
            pltpu.VMEM(r.shape, BF16),
            pltpu.VMEM(k.shape, BF16),
            pltpu.VMEM(rd.shape, BF16),
            pltpu.VMEM(kd.shape, BF16),
            pltpu.VMEM(starts.shape, BF16),
            pltpu.VMEM((3, 1, width), F32),
            pltpu.VMEM((SPAN, width), F32),
            pltpu.VMEM((tail, width), BF16),
            pltpu.VMEM((drafts, width), BF16),
            pltpu.SemaphoreType.DMA((32,)),
            pltpu.SemaphoreType.DMA((PIECES,)),
        ],
        "outputs",
        16 * tail * width * LINE,
        16 * tail * width,
    )


def unpack_kernel(slots, owner, back, state_out, shift_out):
    reqs, lines, width = state_out.shape
    heads = shift_out.shape[2]
    for g in range(reqs // slots):
        rows = back[g].astype(F32)
        for s in range(slots):
            q = owner[g * slots + s]
            mine = rows[s * lines : (s + 1) * lines]
            state_out[q] = mine[:, :width]
            shift_out[q] = mine[:, width : width + heads].astype(BF16)


def unpack(lane_owner, back, slots, lines, width, heads):
    reqs = back.shape[0] * slots
    outs = [((reqs, lines, width), F32), ((reqs, lines, heads), BF16)]
    vmem = pl.BlockSpec(memory_space=pltpu.VMEM)
    return pl.pallas_call(
        functools.partial(unpack_kernel, slots),
        in_specs=[SMEM, vmem],
        out_specs=[vmem, vmem],
        out_shape=[jax.ShapeDtypeStruct(s, t) for s, t in outs],
        compiler_params=params(16),
        name="unpack",
    )(lane_owner, back)


def local(
    groups,
    copies,
    suffix_source,
    suffix_accept,
    suffix_address,
    guess_lane_source,
    guess_lane_accept,
    guess_lane_address,
    content_map,
    forget_shrink_map,
    forget_expand_map,
    forget_lane_anchor,
    present_boost,
    content_blend_share,
    forget_blend_share,
    lane_normal_scale,
    lane_normal_shift,
    kernel_memory_saved,
    prior_source_saved,
    lane_owner,
    request_spans,
    admitted_guesses,
):
    width = content_map.shape[1]
    slots = guess_lane_source.shape[0]
    drafts = slots * DRAFT
    lines = kernel_memory_saved.shape[1]
    line = lambda x: x.reshape(1, width)

    def flip(x, k):
        return lax.ppermute(x, "tp", [(i, i ^ k) for i in range(copies)])

    tail = suffix_source[0]
    keys = suffix_address[0]
    draft_keys = guess_lane_address.reshape(drafts, width)
    mixes = [line(content_blend_share), line(forget_blend_share)]
    cross, near = flip(tail, 2), flip(tail, 1)
    near_mixes = [flip(x, 1) for x in mixes]
    sent = pack(lane_owner, kernel_memory_saved, prior_source_saved, groups)
    got = lax.all_to_all(sent, "rep", 0, 0)
    part_v, part_w = early([tail, near], [*mixes, *near_mixes], forget_shrink_map, content_map)
    got, part_v, part_w = lax.optimization_barrier((got, part_v, part_w))
    owns = own_inputs(got, slots, width)
    small = small_payload(guess_lane_source, tail, *mixes)
    small_cross, small_near = flip(small, 2), flip(small, 1)
    cross, small_cross, owns = lax.optimization_barrier((cross, small_cross, owns))
    owns = [owns] + [flip(owns, k) for k in range(1, copies)]
    far = flip(cross, 1)
    smalls = [small, small_near, small_cross, flip(small_cross, 1)]
    anchor = line(forget_lane_anchor)
    v, low, starts, ret = final(
        (lane_owner, request_spans, admitted_guesses),
        [cross, far],
        smalls,
        owns,
        [part_v, part_w],
        (forget_shrink_map, forget_expand_map, anchor),
        keys,
        draft_keys,
        got,
        content_map,
        slots,
    )
    back = lax.all_to_all(ret, "rep", 0, 0)
    tail_out, draft_out = outputs(
        (lane_owner, request_spans),
        [
            v,
            low,
            forget_expand_map,
            anchor,
            suffix_accept[0],
            keys,
            guess_lane_accept.reshape(drafts, width),
            draft_keys,
            starts,
            line(present_boost),
            line(lane_normal_scale),
            line(lane_normal_shift),
        ],
        slots,
    )
    state_out, shift_out = unpack(lane_owner, back, slots, lines, width, width // SPAN)
    return (
        tail_out[None],
        draft_out.reshape(slots, DRAFT, width),
        state_out,
        shift_out,
    )


def solution(mesh):
    wide = P("rep", None, "tp")
    cached = P(None, "rep", "tp")
    placed = (wide,) * 6 + (P(None, "tp"), P(), P(None, "tp")) + (P("tp"),) * 6
    placed += (cached, cached, P(), P(), P())
    return jax.shard_map(
        functools.partial(local, mesh.shape["rep"], mesh.shape["tp"]),
        mesh=mesh,
        in_specs=placed,
        out_specs=(wide, wide, cached, cached),
        check_vma=False,
    )
```

```python
import functools

import jax
import jax.numpy as jnp
from jax import lax
from jax.experimental import pallas as pl
from jax.experimental.pallas import tpu as pltpu
from jax.sharding import PartitionSpec as P

SPAN = 64
DRAFT = 16
QUAD = 4 * SPAN
PIECES = 3
LINE = 128
EXTRA = 16
TAIL_FIRST, TAIL_LAST, MIX_V, MIX_W = 0, 1, 2, 5
EPS = 0.00064
SAFE = -60.0
F32, BF16 = jnp.float32, jnp.bfloat16
VMEM_MIB = 62
SMEM = pl.BlockSpec(memory_space=pltpu.SMEM)
HBM = pl.BlockSpec(memory_space=pltpu.HBM)


def params(mib=VMEM_MIB):
    return pltpu.CompilerParams(vmem_limit_bytes=mib * 1024 * 1024)


def iota(shape, dim):
    return lax.broadcasted_iota(jnp.int32, shape, dim)


def split2(x, axis):
    high = x.astype(BF16)
    return jnp.concatenate([high, (x - high.astype(F32)).astype(BF16)], axis=axis)


def split3(x):
    high = x.astype(BF16)
    rest = x - high.astype(F32)
    mid = rest.astype(BF16)
    return high, mid, (rest - mid.astype(F32)).astype(BF16)


def dot(a, b):
    return jnp.dot(a, b, preferred_element_type=F32)


def dot_rows(a, b):
    return lax.dot_general(a, b, (((0,), (0,)), ((), ())), preferred_element_type=F32)


def dot_lanes(a, b):
    return lax.dot_general(a, b, (((1,), (1,)), ((), ())), preferred_element_type=F32)


def quad_lanes(p):
    if isinstance(p, int):
        return slice(p * QUAD, (p + 1) * QUAD)
    return pl.ds(pl.multiple_of(p * QUAD, QUAD), QUAD)


class Copies:
    def __init__(self, sems):
        self.sems, self.used = sems, 0

    def start(self, source, target):
        copy = pltpu.make_async_copy(source, target, self.sems.at[self.used])
        self.used += 1
        copy.start()
        return copy


def call(kernel, args, in_specs, outs, scratch, name, flops=0, moved=0, out_specs=None, mib=VMEM_MIB):
    return pl.pallas_call(
        kernel,
        in_specs=in_specs,
        out_specs=out_specs or [HBM] * len(outs),
        out_shape=[jax.ShapeDtypeStruct(s, t) for s, t in outs],
        scratch_shapes=scratch,
        compiler_params=params(mib),
        cost_estimate=pl.CostEstimate(flops=flops, bytes_accessed=moved, transcendentals=0),
        name=name,
    )(*args)


def pack_kernel(slots, owner, state, prior, out, held, cached, lines, sems):
    groups, rows, _ = out.shape
    width = state.shape[2]
    heads = prior.shape[2]
    go = Copies(sems)
    second = go.start(state, held)
    first = go.start(prior, cached)
    lines[...] = jnp.zeros_like(lines)
    first.wait()
    lines[:, :, 0:heads] = cached[...].astype(F32)
    second.wait()
    for g in range(groups):
        reqs = [owner[g * slots + s] for s in range(slots)]
        out[g, :, 0:width] = jnp.concatenate([held[q] for q in reqs], axis=0).astype(BF16)
        out[g, :, width:] = jnp.concatenate([lines[q] for q in reqs], axis=0).astype(BF16)


def pack(lane_owner, state, prior, groups):
    reqs, depth, width = state.shape
    slots = reqs // groups
    out = (groups, slots * depth, width + LINE)
    return pl.pallas_call(
        functools.partial(pack_kernel, slots),
        grid=(1,),
        in_specs=[SMEM, HBM, HBM],
        out_specs=pl.BlockSpec(out, lambda i: (0, 0, 0)),
        out_shape=jax.ShapeDtypeStruct(out, BF16),
        scratch_shapes=[
            pltpu.VMEM(state.shape, F32),
            pltpu.VMEM(prior.shape, BF16),
            pltpu.VMEM((reqs, depth, LINE), F32),
            pltpu.SemaphoreType.DMA((2,)),
        ],
        compiler_params=params(),
        name="pack",
    )(lane_owner, state, prior)


def small_kernel(slots, draft, tail, mix_v, mix_w, small, ends, shares, held, sems):
    copies = Copies(sems)
    last = tail.shape[0] - 16
    drafts = slots * DRAFT
    width = held.shape[1]
    waits = [
        copies.start(tail.at[pl.ds(0, 16), :], ends.at[0]),
        copies.start(tail.at[pl.ds(last, 16), :], ends.at[1]),
        copies.start(mix_v, shares.at[0]),
        copies.start(mix_w, shares.at[1]),
    ]
    waits += [copies.start(draft.at[s], held.at[pl.ds(s * DRAFT, DRAFT), :]) for s in range(slots)]
    row = iota((EXTRA, width), 0)
    for w in waits:
        w.wait()
    value = jnp.where(row == TAIL_FIRST, ends[0].astype(F32)[0:1], 0.0)
    value = jnp.where(row == TAIL_LAST, ends[1].astype(F32)[15:16], value)
    for n, base in enumerate((MIX_V, MIX_W)):
        for m, part in enumerate(split3(shares[n])):
            value = jnp.where(row == base + m, part.astype(F32), value)
    held[drafts:, :] = value.astype(BF16)
    copies.start(held, small).wait()


def small_payload(draft, tail, mix_v, mix_w):
    slots, _, width = draft.shape
    size = (slots * DRAFT + EXTRA, width)
    return call(
        functools.partial(small_kernel, slots),
        (draft, tail, mix_v, mix_w),
        [HBM] * 4,
        [(size, BF16)],
        [
            pltpu.VMEM((2, 16, width), BF16),
            pltpu.VMEM((2, 1, width), F32),
            pltpu.VMEM(size, BF16),
            pltpu.SemaphoreType.DMA((5 + slots,)),
        ],
        "small_payload",
    )[0]


def head_ones(scale=1.0):
    r, c = iota((QUAD, QUAD), 0), iota((QUAD, QUAD), 1)
    return jnp.where(r // SPAN == c // SPAN, scale, 0.0).astype(BF16)


def head_masks(dtype):
    lane = iota((1, QUAD), 1) // SPAN
    return [(lane == h).astype(F32).astype(dtype) for h in range(QUAD // SPAN)]


def by_head(x, masks):
    return jnp.concatenate([x * m for m in masks], axis=0)


def own_rows(x, depth):
    lane = iota((depth, QUAD), 1) // SPAN
    out = x[:depth]
    for h in range(1, QUAD // SPAN):
        out = jnp.where(lane == h, x[h * depth : (h + 1) * depth], out)
    return out


def down_state(line, ones):
    keep = iota((SPAN, QUAD), 0) == iota((SPAN, QUAD), 1) % SPAN
    both = dot(split2(jnp.where(keep, line, 0.0), 0), ones)
    return both[:SPAN] + both[SPAN:]


def gathered(keys, v):
    return own_rows(dot_rows(keys.astype(BF16), v), SPAN)


def sums_after(n):
    t, u = iota((n, 2 * n), 0), iota((n, 2 * n), 1) & (n - 1)
    return (u > t).astype(BF16)


def mixed(x, previous, share):
    return (x + (previous - x) * share).astype(BF16)


def shares_of(rest):
    take = lambda n: rest[n : n + 1] + rest[n + 1 : n + 2] + rest[n + 2 : n + 3]
    return take(MIX_V), take(MIX_W)


def draft_mixes(d, owns, is_long, slots):
    drafts = slots * DRAFT
    rest = d[drafts:]
    share_v, share_w = shares_of(rest)
    row = iota(d.shape, 0)
    previous = pltpu.roll(d, 1, 0)
    for s in range(slots):
        own = owns[s : s + 1]
        first = jnp.where(is_long[s], rest[TAIL_LAST : TAIL_LAST + 1], own)
        previous = jnp.where(row == s * DRAFT, first, previous)
        if s == 0:
            previous = jnp.where(row == drafts + TAIL_FIRST, own, previous)
    return mixed(d, previous, share_v), mixed(d, previous, share_w), share_v, share_w


def long_slots(owner, spans, slots):
    first = lax.axis_index("rep") * slots
    return [spans[owner[first + s]] > DRAFT for s in range(slots)]


def feature_block(j, width):
    return pl.ds(pl.multiple_of(jnp.bitwise_xor(lax.axis_index("tp"), j) * width, width), width)


def early_kernel(*refs):
    refs = list(refs)
    take = lambda n: [refs.pop(0) for _ in range(n)]
    xs_in, shares_in = take(2), take(4)
    shrink_in, weights = take(2)
    v_out, w_out, xs, shares, shrink, held, acc_v, acc_w, sems = take(9)
    width = xs.shape[2]
    go = Copies(sems)
    waits = []
    for j in range(2):
        block = feature_block(j, width)
        waits.append(
            [
                go.start(shares_in[2 * j], shares.at[2 * j]),
                go.start(shares_in[2 * j + 1], shares.at[2 * j + 1]),
                go.start(xs_in[j], xs.at[j]),
                go.start(shrink_in.at[block, :], shrink.at[j]),
                go.start(weights.at[block, :], held.at[j]),
            ]
        )
    for j in range(2):
        for w in waits[j]:
            w.wait()
        x = xs[j].astype(F32)
        previous = pltpu.roll(x, 1, 0)
        low = dot(mixed(x, previous, shares[2 * j + 1]), shrink[j])
        part = dot(mixed(x, previous, shares[2 * j]), held[j])
        if j == 0:
            acc_w[...] = low
            acc_v[...] = part
        else:
            acc_w[...] += low
            acc_v[...] += part
    outs = [go.start(acc_v, v_out), go.start(acc_w, w_out)]
    for w in outs:
        w.wait()


def early(xs, shares, shrink, weights):
    rows, width = xs[0].shape
    rank = shrink.shape[1]
    return call(
        early_kernel,
        (*xs, *shares, shrink, weights),
        [HBM] * 8,
        [((rows, width), F32), ((rows, rank), F32)],
        [
            pltpu.VMEM((2, rows, width), BF16),
            pltpu.VMEM((4, 1, width), F32),
            pltpu.VMEM((2, width, rank), BF16),
            pltpu.VMEM((2, width, width), BF16),
            pltpu.VMEM((rows, width), F32),
            pltpu.VMEM((rows, rank), F32),
            pltpu.SemaphoreType.DMA((12,)),
        ],
        "early",
        4 * rows * width * width,
        4 * width * width,
    )


def owns_kernel(slots, got_in, out, lines, held, sems):
    width = out.shape[1]
    copy = pltpu.make_async_copy(got_in.at[:, :, pl.ds(width, LINE)], lines, sems.at[0])
    copy.start()
    place = (iota((LINE, width), 0) == iota((LINE, width), 1) // SPAN).astype(BF16)
    keep = iota((SPAN, width), 0) == iota((SPAN, width), 1) % SPAN
    row = iota((EXTRA, width), 0)
    groups, per, _ = lines.shape
    depth = per // slots
    copy.wait()
    wide = lines[...].astype(F32)
    value = jnp.zeros((EXTRA, width), F32)
    for s in range(slots):
        mine = [wide[g, s * depth : (s + 1) * depth] for g in range(groups)]
        spread = dot(jnp.concatenate(mine, axis=0).astype(BF16), place)
        own = jnp.sum(jnp.where(keep, spread, 0.0), axis=0, keepdims=True)
        value = jnp.where(row == s, own, value)
    held[...] = value.astype(BF16)
    copy = pltpu.make_async_copy(held, out, sems.at[1])
    copy.start()
    copy.wait()


def own_inputs(got, slots, width):
    return call(
        functools.partial(owns_kernel, slots),
        (got,),
        [HBM],
        [((EXTRA, width), BF16)],
        [
            pltpu.VMEM((got.shape[0], got.shape[1], LINE), BF16),
            pltpu.VMEM((EXTRA, width), BF16),
            pltpu.SemaphoreType.DMA((2,)),
        ],
        "own_inputs",
        mib=8,
    )[0]


def final_kernel(slots, copies, direct, *refs):
    refs = list(refs)
    take = lambda n: [refs.pop(0) for _ in range(n)]
    owner, spans, admitted = take(3)
    xs_in, smalls_in, owns_in, parts_in = take(2), take(copies), take(copies), take(2)
    shrink_in, expand_in, anchor_in, keys_in, draft_keys_in, got_in, weights = take(7)
    v_out, low_out, starts_out, back = take(4)
    xs, smalls, owns, part_v, part_w, shrink, expand, anchor, keys, draft_keys, got, held = take(12)
    v_held, w_held, low_held, starts, sems = take(5)

    tail, width = xs.shape[1:]
    rows = tail // PIECES
    quads = width // QUAD
    drafts = slots * DRAFT
    groups = got.shape[0]
    lines = SPAN // groups
    special = tail + drafts
    go = Copies(sems)
    blocks = [feature_block(j, width) for j in range(copies)]
    wait_small = [go.start(smalls_in[j], smalls.at[j]) for j in range(copies)]
    wait_small += [go.start(owns_in[j], owns.at[j]) for j in range(copies)]
    wait_x, wait_w = [], {}
    for n in range(2):
        wait_x.append(go.start(xs_in[n], xs.at[n]))
        if n == 0:
            wait_shrink = go.start(shrink_in, shrink)
        wait_w[2 + n] = go.start(weights.at[blocks[2 + n], :], held.at[2 + n])
    for j in range(2):
        wait_w[j] = go.start(weights.at[blocks[j], :], held.at[j])
    wait_part = [go.start(parts_in[0], part_v), go.start(parts_in[1], part_w)]
    wait_part += [go.start(expand_in, expand), go.start(anchor_in, anchor)]
    wait_keys = [go.start(keys_in, keys), go.start(draft_keys_in, draft_keys), go.start(got_in, got)]
    is_long = long_slots(owner, spans, slots)
    first_slot = lax.axis_index("rep") * slots
    counts = [admitted[owner[first_slot + s]] for s in range(slots)]

    for w in wait_small:
        w.wait()

    def drafts_of(j):
        return draft_mixes(smalls[j].astype(F32), owns[j].astype(F32), is_long, slots)

    acc_v = acc_w = None
    for n in range(2):
        dv, dw, share_v, share_w = drafts_of(2 + n)
        wait_x[n].wait()
        now = xs[n].astype(F32)
        previous = pltpu.roll(now, 1, 0)
        xv = jnp.concatenate([mixed(now, previous, share_v), dv], axis=0)
        xw = jnp.concatenate([mixed(now, previous, share_w), dw], axis=0)
        if n == 0:
            wait_shrink.wait()
        low = dot(xw, shrink[blocks[2 + n], :])
        wait_w[2 + n].wait()
        part = dot(xv, held[2 + n])
        acc_w = low if n == 0 else acc_w + low
        acc_v = part if n == 0 else acc_v + part
    draft_v, draft_w = acc_v[tail:], acc_w[tail:]
    for j in range(2):
        dv, dw, _, _ = drafts_of(j)
        draft_w = draft_w + dot(dw, shrink[blocks[j], :])
        wait_w[j].wait()
        draft_v = draft_v + dot(dv, held[j])
    for w in wait_part:
        w.wait()
    v_held[0:tail, :] = (acc_v[:tail] + part_v[...]).astype(BF16)
    v_held[tail:, :] = draft_v.astype(BF16)
    acc_w = jnp.concatenate([acc_w[:tail] + part_w[...], draft_w], axis=0)
    low_held[...] = jnp.tanh(acc_w).astype(BF16)
    rate = -jnp.exp(anchor[...] + dot(low_held[...], expand[...]))
    w_held[0:8, :] = jnp.where(iota((8, width), 0) == 0, 0.0, rate[:8])
    w_held[8:, :] = rate[8:]
    outs = [go.start(v_held, v_out), go.start(low_held, low_out)]
    for w in wait_keys:
        w.wait()

    ones = head_ones()
    after = sums_after(rows)
    t, u = iota((drafts, 2 * drafts), 0), iota((drafts, 2 * drafts), 1) & (drafts - 1)
    limit = jnp.zeros(t.shape, jnp.int32)
    row, row_limit = iota((drafts, QUAD), 0), jnp.zeros((drafts, QUAD), jnp.int32)
    for s in range(slots):
        limit = jnp.where((t >= s * DRAFT) & (t < (s + 1) * DRAFT), s * DRAFT + counts[s], limit)
        row_limit = jnp.where(
            (row >= s * DRAFT) & (row < (s + 1) * DRAFT), s * DRAFT + counts[s], row_limit
        )
    draft_after = ((u > t) & (u < limit)).astype(BF16)
    taken = row < row_limit
    for p in range(quads):
        lanes = quad_lanes(p)
        parts, rest = [], jnp.zeros((1, QUAD), F32)
        for n in reversed(range(PIECES)):
            w = w_held[n * rows : (n + 1) * rows, lanes]
            k = keys[n * rows : (n + 1) * rows, lanes].astype(F32)
            k = k * jnp.exp(dot(after, split2(w, 0)) + rest)
            if n == 0:
                k = jnp.where(iota(k.shape, 0) == 0, 0.0, k)
            parts.append(k)
            rest = rest + jnp.sum(w, axis=0, keepdims=True)
        gained = gathered(jnp.concatenate(parts[::-1], axis=0), v_held[0:tail, lanes])
        begin = [
            jnp.concatenate(
                [got[g, :, lanes].astype(F32)[s * lines : (s + 1) * lines] for g in range(groups)], axis=0
            )
            for s in range(slots)
        ]
        starts[0, :, lanes] = begin[0].astype(BF16)
        lift = jnp.exp(down_state(w_held[special : special + 1, lanes], ones))
        key = down_state(keys[0:16, lanes].astype(F32)[0:1], ones)
        state = lift * begin[0] + key * v_held[special : special + 16, lanes].astype(F32)[0:1]
        starts[1, :, lanes] = state.astype(BF16)
        state = jnp.exp(down_state(rest, ones)) * state + gained
        begin[0] = jnp.where(is_long[0], state, begin[0])
        w = w_held[tail:special, lanes]
        k = draft_keys[:, lanes].astype(F32) * jnp.exp(dot(draft_after, split2(w, 0)))
        k = jnp.where(taken, k, 0.0)
        v = v_held[tail:special, lanes]
        closed = []
        for s in range(slots):
            starts[2 + s, :, lanes] = begin[s].astype(BF16)
            mine = slice(s * DRAFT, (s + 1) * DRAFT)
            upto = jnp.sum(jnp.where(taken[mine], w[mine], 0.0), axis=0, keepdims=True)
            closed.append(jnp.exp(down_state(upto, ones)) * begin[s] + gathered(k[mine], v[mine]))
        if direct:
            for g in range(groups):
                part = jnp.concatenate([c[g * lines : (g + 1) * lines] for c in closed], axis=0)
                back[g, :, lanes] = part.astype(BF16)
        else:
            for s in range(slots):
                back[s, :, lanes] = closed[s].astype(BF16)
    outs.append(go.start(starts, starts_out))

    tokens = smalls[0].astype(F32)
    row = iota(tokens.shape, 0)
    place = (iota((LINE, width), 0) == iota((LINE, width), 1) // SPAN).astype(BF16)
    keep = iota((SPAN, width), 0) == iota((SPAN, width), 1) % SPAN
    edges = []
    for s in range(slots):
        own = owns[0].astype(F32)[s : s + 1]
        first = jnp.where(is_long[s], tokens[drafts + TAIL_LAST : drafts + TAIL_LAST + 1], own)
        chosen = jnp.sum(
            jnp.where(row == s * DRAFT + counts[s] - 1, tokens, 0.0), axis=0, keepdims=True
        )
        edge = jnp.where(counts[s] > 0, chosen, first)
        edges.append(dot_lanes(jnp.where(keep, edge, 0.0).astype(BF16), place))
    if direct:
        for g in range(groups):
            part = jnp.concatenate([e[g * lines : (g + 1) * lines] for e in edges], axis=0)
            back[g, :, width:] = part.astype(BF16)
    else:
        for s in range(slots):
            back[s, :, width:] = edges[s].astype(BF16)
    for w in outs:
        w.wait()


def final(scalars, xs, smalls, owns, parts, maps, keys, draft_keys, got, weights, slots):
    tail, width = xs[0].shape
    total = tail + smalls[0].shape[0]
    copies = len(smalls)
    groups = got.shape[0]
    rank = maps[0].shape[1]
    direct = SPAN // groups == 8
    back = (groups, got.shape[1]) if direct else (slots, SPAN)
    back = (*back, width + LINE)
    starts = (2 + slots, SPAN, width)
    args = [*scalars, *xs, *smalls, *owns, *parts, *maps, keys, draft_keys, got, weights]
    v, low, begins, ret = call(
        functools.partial(final_kernel, slots, copies, direct),
        args,
        [SMEM] * len(scalars) + [HBM] * (len(args) - len(scalars)),
        [((total, width), BF16), ((total, rank), BF16), (starts, BF16), (back, BF16)],
        [
            pltpu.VMEM((2, tail, width), BF16),
            pltpu.VMEM((copies, *smalls[0].shape), BF16),
            pltpu.VMEM((copies, *owns[0].shape), BF16),
            pltpu.VMEM((tail, width), F32),
            pltpu.VMEM((tail, rank), F32),
            pltpu.VMEM(maps[0].shape, BF16),
            pltpu.VMEM(maps[1].shape, BF16),
            pltpu.VMEM((1, width), F32),
            pltpu.VMEM(keys.shape, BF16),
            pltpu.VMEM(draft_keys.shape, BF16),
            pltpu.VMEM(got.shape, BF16),
            pltpu.VMEM((copies, width, width), BF16),
            pltpu.VMEM((total, width), BF16),
            pltpu.VMEM((total, width), F32),
            pltpu.VMEM((total, rank), BF16),
            pltpu.VMEM(starts, BF16),
            pltpu.SemaphoreType.DMA((32,)),
        ],
        "final",
        4 * tail * width * width,
        4 * width * width,
        [HBM, HBM, HBM, pl.BlockSpec(memory_space=pltpu.VMEM)],
    )
    if not direct:
        ret = ret.reshape(slots, groups, SPAN // groups, width + LINE).transpose(1, 0, 2, 3)
        ret = ret.reshape(groups, slots * SPAN // groups, width + LINE)
    return v, low, begins, ret


def levels_scores(r, k, rate, length, masks):
    n = r.shape[0]
    heads = len(masks)
    pieces = jnp.concatenate(split3(rate), axis=0)

    def level(n_level, total):
        half = lax.shift_left(jnp.int32(1), n_level)
        shift = n_level + 1
        t, u = iota((n, 3 * n), 0), iota((n, 3 * n), 1) % n
        edge = lax.shift_left(lax.shift_right_logical(t, shift), shift) + half
        after = (t >= edge) & (u >= edge) & (u < t)
        ahead = (t < edge) & (u > t) & (u < edge)
        decay = jnp.exp(dot((after | ahead).astype(BF16), pieces))
        row = iota(r.shape, 0)
        row_edge = lax.shift_left(lax.shift_right_logical(row, shift), shift) + half
        rt = jnp.where(row >= row_edge, r * decay, 0.0).astype(BF16)
        kt = jnp.where(row < row_edge, k * decay, 0.0)
        sc = dot_lanes(rt, by_head(kt, masks).astype(BF16))
        t2, s2 = iota((n, heads * n), 0), iota((n, heads * n), 1) & (n - 1)
        same = lax.shift_right_logical(t2, shift) == lax.shift_right_logical(s2, shift)
        return total + jnp.where(same, sc, 0.0)

    start = jnp.zeros((n, heads * n), F32)
    return lax.fori_loop(0, length.bit_length() - 1, level, start)


def answers(r, k, v, rate, boost, states, length, scaled, ones, masks):
    n = r[0].shape[0]
    count = n // length
    heads = len(masks)
    every = range(len(r))
    t, u = iota((n, 2 * n), 0), iota((n, 2 * n), 1) & (n - 1)
    t2, s2 = iota((n, heads * n), 0), iota((n, heads * n), 1) & (n - 1)
    earlier, keep = u < t, s2 < t2
    if count > 1:
        earlier = earlier & (u // length == t // length)
        keep = keep & (s2 // length == t2 // length)
    earlier = earlier.astype(BF16)
    before = [dot(earlier, split2(x, 0)) for x in rate]
    if scaled:
        middle = []
        for x in before:
            rows = [x[s * length + length // 2 :][:1] for s in range(count)]
            if count > 1:
                rows = [jnp.concatenate([jnp.broadcast_to(m, (length, QUAD)) for m in rows], axis=0)]
            middle.append(rows[0])
        rt = [(r[i] * jnp.exp(before[i] - middle[i])).astype(BF16) for i in every]
        kt = [(k[i] * jnp.exp(middle[i] - before[i] - rate[i])).astype(BF16) for i in every]
        sc = [dot_lanes(rt[i], by_head(kt[i], masks)) for i in every]
        sc = [jnp.where(keep, x, 0.0).astype(BF16) for x in sc]
    else:
        sc = [levels_scores(r[i], k[i], rate[i], length, masks).astype(BF16) for i in every]
    bonus = [dot((r[i] * k[i] * boost[i]).astype(BF16), ones) * v[i].astype(F32) for i in every]
    rs = [(r[i] * jnp.exp(before[i])).astype(BF16) for i in every]
    y = [dot(sc[i], by_head(v[i], masks)) + bonus[i] for i in every]
    for i in every:
        outer = [
            dot(rs[i][s * length : (s + 1) * length], by_head(states[i][s], masks))
            for s in range(count)
        ]
        y[i] = y[i] + (outer[0] if count == 1 else jnp.concatenate(outer, axis=0))
    return y


def normed(y, gain, bias, mean_ones):
    every = range(len(y))
    center = [x - dot(x.astype(BF16), mean_ones) for x in y]
    spread = [dot((x * x).astype(BF16), mean_ones) for x in center]
    return [
        (center[i] * lax.rsqrt(spread[i] + EPS) * gain[i] + bias[i]).astype(BF16) for i in every
    ]


def outputs_kernel(slots, *refs):
    refs = list(refs)
    take = lambda n: [refs.pop(0) for _ in range(n)]
    owner, spans = take(2)
    v_in, low_in, expand_in, anchor_in, r_in, k_in, rd_in, kd_in, starts_in = take(9)
    lines_in = take(3)
    tail_out, draft_out = take(2)
    low, expand, anchor, v_held, w_held, r_held, k_held, rd, kd, starts, lines, states, out_held, draft_held, sems, done = take(16)
    tail, width = out_held.shape
    rows = tail // PIECES
    quads = width // QUAD
    drafts = slots * DRAFT
    special = tail + drafts
    go = Copies(sems)
    is_long = spans[owner[lax.axis_index("rep") * slots]] > DRAFT

    def leaving(n):
        at = pl.ds(n * rows, rows)
        return pltpu.make_async_copy(out_held.at[at, :], tail_out.at[at, :], done.at[n])

    def send(n):
        leaving(n).start()

    late = pl.ds(tail, drafts + EXTRA)
    wait_rate = [go.start(low_in, low), go.start(expand_in, expand), go.start(anchor_in, anchor)]
    waits = [go.start(v_in.at[late, :], v_held.at[late, :])]
    waits += [go.start(rd_in, rd), go.start(kd_in, kd), go.start(starts_in, starts)]
    waits += [go.start(x, lines.at[n]) for n, x in enumerate(lines_in)]
    pieces = [pl.ds(n * rows, rows) for n in range(PIECES)]
    loads = []
    for at in pieces:
        loads.append(
            [
                go.start(r_in.at[at, :], r_held.at[at, :]),
                go.start(k_in.at[at, :], k_held.at[at, :]),
                go.start(v_in.at[at, :], v_held.at[at, :]),
            ]
        )
    ones, mean_ones = head_ones(), head_ones(1.0 / SPAN)
    masks = head_masks(BF16)
    for w in wait_rate:
        w.wait()
    rate = -jnp.exp(anchor[...] + dot(low[...], expand[...]))
    w_held[0:8, :] = jnp.where(iota((8, width), 0) == 0, 0.0, rate[:8])
    w_held[8:, :] = rate[8:]
    for w in waits:
        w.wait()

    def line(n, lanes):
        return lines[n, :, lanes]

    def draft_quads(which, scaled):
        lanes = [quad_lanes(p) for p in which]
        y = answers(
            [rd[:, at].astype(F32) for at in lanes],
            [kd[:, at].astype(F32) for at in lanes],
            [v_held[tail:special, at] for at in lanes],
            [w_held[tail:special, at] for at in lanes],
            [line(0, at) for at in lanes],
            [[starts[2 + s, :, at] for s in range(slots)] for at in lanes],
            DRAFT, scaled, ones, masks,
        )
        out = normed(y, [line(1, at) for at in lanes], [line(2, at) for at in lanes], mean_ones)
        for at, x in zip(lanes, out):
            draft_held[:, at] = x

    sums = [
        jnp.sum(w_held[tail + s * DRAFT : tail + (s + 1) * DRAFT, :], axis=0, keepdims=True)
        for s in range(slots)
    ]
    safe = jnp.min(jnp.concatenate(sums, axis=0)) > SAFE

    @pl.when(safe)
    def _():
        draft_quads(range(quads), True)

    @pl.when(jnp.logical_not(safe))
    def _():
        def body(p, carry):
            draft_quads([p], False)
            return carry

        lax.fori_loop(0, quads, body, 0)

    out_waits = [go.start(draft_held, draft_out)]

    def tail_quads(n, which, scaled, carry_on):
        lanes = [quad_lanes(p) for p in which]
        every = range(len(lanes))
        at = pieces[n] if isinstance(n, int) else pl.ds(pl.multiple_of(n * rows, rows), rows)
        r = [r_held[at, x].astype(F32) for x in lanes]
        k = [k_held[at, x].astype(F32) for x in lanes]
        v = [v_held[at, x] for x in lanes]
        rate = [w_held[at, x] for x in lanes]
        state = [states[:, x] for x in lanes]
        boost = [line(0, x) for x in lanes]
        zr, zk = r, k
        if not isinstance(n, int) or n == 0:
            first = (iota((rows, QUAD), 0) == 0) & (n == 0)
            zr, zk = [jnp.where(first, 0.0, x) for x in r], [jnp.where(first, 0.0, x) for x in k]
        y = answers(
            zr, zk, v, rate, boost, [[x.astype(BF16)] for x in state], rows, scaled, ones, masks
        )
        if not isinstance(n, int) or n == 0:
            for i in every:
                r0, k0 = r[i][0:8], k[i][0:8]
                v0 = v_held[special : special + EXTRA, lanes[i]].astype(F32)[0:1]
                y0 = dot(r0.astype(BF16), by_head(starts[0, :, lanes[i]], masks))
                y0 = y0 + dot((r0 * k0 * boost[i]).astype(BF16), ones) * v0
                y[i] = jnp.where(first, y0[0:1], y[i])
        out = normed(y, [line(1, x) for x in lanes], [line(2, x) for x in lanes], mean_ones)
        for i in every:
            out_held[at, lanes[i]] = out[i]
        if carry_on:
            after = sums_after(rows)
            kept = [down_state(jnp.sum(x, axis=0, keepdims=True), ones) for x in rate]
            late = [dot(after, split2(x, 0)) for x in rate]
            gain = [gathered(zk[i] * jnp.exp(late[i]), v[i]) for i in every]
            for i in every:
                states[:, lanes[i]] = jnp.exp(kept[i]) * state[i] + gain[i]

    @pl.when(is_long)
    def _():
        states[...] = starts[1].astype(F32)
        lowest = functools.reduce(
            jnp.minimum,
            [
                jnp.sum(w_held[n * rows : (n + 1) * rows, :], axis=0, keepdims=True)
                for n in range(PIECES)
            ],
        )
        fine = jnp.min(lowest) > SAFE

        @pl.when(fine)
        def _():
            for n in range(PIECES):
                for w in loads[n]:
                    w.wait()
                tail_quads(n, range(quads), True, n < PIECES - 1)
                send(n)

        @pl.when(jnp.logical_not(fine))
        def _():
            for group in loads:
                for w in group:
                    w.wait()

            def body(m, carry):
                tail_quads(m // quads, [m % quads], False, True)
                return carry

            lax.fori_loop(0, PIECES * quads, body, 0)
            for n in range(PIECES):
                send(n)

    @pl.when(jnp.logical_not(is_long))
    def _():
        for group in loads:
            for w in group:
                w.wait()
        out_held[...] = jnp.zeros_like(out_held)
        for n in range(PIECES):
            send(n)

    for w in out_waits:
        w.wait()
    for n in range(PIECES):
        leaving(n).wait()


def outputs(scalars, arrays, slots):
    v, low, expand, anchor, r, k, rd, kd, starts = arrays[:9]
    tail, width = r.shape
    drafts = slots * DRAFT
    args = [*scalars, *arrays]
    return call(
        functools.partial(outputs_kernel, slots),
        args,
        [SMEM] * len(scalars) + [HBM] * (len(args) - len(scalars)),
        [((tail, width), BF16), ((drafts, width), BF16)],
        [
            pltpu.VMEM(low.shape, BF16),
            pltpu.VMEM(expand.shape, BF16),
            pltpu.VMEM(anchor.shape, F32),
            pltpu.VMEM(v.shape, BF16),
            pltpu.VMEM(v.shape, F32),
            pltpu.VMEM(r.shape, BF16),
            pltpu.VMEM(k.shape, BF16),
            pltpu.VMEM(rd.shape, BF16),
            pltpu.VMEM(kd.shape, BF16),
            pltpu.VMEM(starts.shape, BF16),
            pltpu.VMEM((3, 1, width), F32),
            pltpu.VMEM((SPAN, width), F32),
            pltpu.VMEM((tail, width), BF16),
            pltpu.VMEM((drafts, width), BF16),
            pltpu.SemaphoreType.DMA((32,)),
            pltpu.SemaphoreType.DMA((PIECES,)),
        ],
        "outputs",
        16 * tail * width * LINE,
        16 * tail * width,
    )


def unpack_kernel(slots, owner, back, state_out, shift_out):
    reqs, lines, width = state_out.shape
    heads = shift_out.shape[2]
    for g in range(reqs // slots):
        rows = back[g].astype(F32)
        for s in range(slots):
            q = owner[g * slots + s]
            mine = rows[s * lines : (s + 1) * lines]
            state_out[q] = mine[:, :width]
            shift_out[q] = mine[:, width : width + heads].astype(BF16)


def unpack(lane_owner, back, slots, lines, width, heads):
    reqs = back.shape[0] * slots
    outs = [((reqs, lines, width), F32), ((reqs, lines, heads), BF16)]
    vmem = pl.BlockSpec(memory_space=pltpu.VMEM)
    return pl.pallas_call(
        functools.partial(unpack_kernel, slots),
        in_specs=[SMEM, vmem],
        out_specs=[vmem, vmem],
        out_shape=[jax.ShapeDtypeStruct(s, t) for s, t in outs],
        compiler_params=params(16),
        name="unpack",
    )(lane_owner, back)


def local(
    groups,
    copies,
    suffix_source,
    suffix_accept,
    suffix_address,
    guess_lane_source,
    guess_lane_accept,
    guess_lane_address,
    content_map,
    forget_shrink_map,
    forget_expand_map,
    forget_lane_anchor,
    present_boost,
    content_blend_share,
    forget_blend_share,
    lane_normal_scale,
    lane_normal_shift,
    kernel_memory_saved,
    prior_source_saved,
    lane_owner,
    request_spans,
    admitted_guesses,
):
    width = content_map.shape[1]
    slots = guess_lane_source.shape[0]
    drafts = slots * DRAFT
    lines = kernel_memory_saved.shape[1]
    line = lambda x: x.reshape(1, width)

    def flip(x, k):
        return lax.ppermute(x, "tp", [(i, i ^ k) for i in range(copies)])

    tail = suffix_source[0]
    keys = suffix_address[0]
    draft_keys = guess_lane_address.reshape(drafts, width)
    mixes = [line(content_blend_share), line(forget_blend_share)]
    cross, near = flip(tail, 2), flip(tail, 1)
    near_mixes = [flip(x, 1) for x in mixes]
    sent = pack(lane_owner, kernel_memory_saved, prior_source_saved, groups)
    got = lax.all_to_all(sent, "rep", 0, 0)
    part_v, part_w = early([tail, near], [*mixes, *near_mixes], forget_shrink_map, content_map)
    got, part_v, part_w = lax.optimization_barrier((got, part_v, part_w))
    owns = own_inputs(got, slots, width)
    small = small_payload(guess_lane_source, tail, *mixes)
    small_cross, small_near = flip(small, 2), flip(small, 1)
    cross, small_cross, owns = lax.optimization_barrier((cross, small_cross, owns))
    owns = [owns] + [flip(owns, k) for k in range(1, copies)]
    far = flip(cross, 1)
    smalls = [small, small_near, small_cross, flip(small_cross, 1)]
    anchor = line(forget_lane_anchor)
    v, low, starts, ret = final(
        (lane_owner, request_spans, admitted_guesses),
        [cross, far],
        smalls,
        owns,
        [part_v, part_w],
        (forget_shrink_map, forget_expand_map, anchor),
        keys,
        draft_keys,
        got,
        content_map,
        slots,
    )
    back = lax.all_to_all(ret, "rep", 0, 0)
    tail_out, draft_out = outputs(
        (lane_owner, request_spans),
        [
            v,
            low,
            forget_expand_map,
            anchor,
            suffix_accept[0],
            keys,
            guess_lane_accept.reshape(drafts, width),
            draft_keys,
            starts,
            line(present_boost),
            line(lane_normal_scale),
            line(lane_normal_shift),
        ],
        slots,
    )
    state_out, shift_out = unpack(lane_owner, back, slots, lines, width, width // SPAN)
    return (
        tail_out[None],
        draft_out.reshape(slots, DRAFT, width),
        state_out,
        shift_out,
    )


def solution(mesh):
    wide = P("rep", None, "tp")
    cached = P(None, "rep", "tp")
    placed = (wide,) * 6 + (P(None, "tp"), P(), P(None, "tp")) + (P("tp"),) * 6
    placed += (cached, cached, P(), P(), P())
    return jax.shard_map(
        functools.partial(local, mesh.shape["rep"], mesh.shape["tp"]),
        mesh=mesh,
        in_specs=placed,
        out_specs=(wide, wide, cached, cached),
        check_vma=False,
    )
```
